32 devices in a mesh: dp: 8 (over z, core), ns: 4 (over y, x).
Axes of the slice: x: 2, y: 2, z: 4, core: 2. Of those that a mesh axis runs over, the one named last changes fastest.
Arguments:
- frames: bfloat16 [2, 128, 121, 2048], P(None, ('dp', 'ns')), may hold values from -9 to 9
- game_ids: int32 [2, 128, 1], P(None, ('dp', 'ns')), may hold values from 0 to 7; in each aligned block of 16 rows (0 to 15, 16 to 31, ..., all dimensions but the last counted through in order) at most 4 rows name the same one
- actions: int32 [2, 128], P(None, ('dp', 'ns')), may hold values from 0 to 17
- groups: int32 [2, 128], P(None, ('dp', 'ns')), may hold values from 0 to 1
- targets: bfloat16 [2, 128], P(None, ('dp', 'ns')), may hold values from -1.796875 to 1.796875
- w_pair: float32 [2, 2, 2048, 512], P(None, None, 'ns'), may hold values from -0.125 to 0.125
- w_spatial: float32 [2, 4608, 512], P(None, 'ns'), may hold values from -0.09375 to 0.09375
- mom_pair: float32 [2, 2, 2048, 512], P(None, None, 'ns'), may hold values from -1.8384316e-05 to 1.8384316e-05
- mom_spatial: float32 [2, 4608, 512], P(None, 'ns'), may hold values from -1.8384316e-05 to 1.8384316e-05
- head_table: float32 [8, 2048, 918], P('dp', 'ns'), may hold values from -0.375 to 0.375
- head_first: float32 [8, 2048, 918], P('dp', 'ns'), may hold values from -1.1444092e-05 to 1.1444092e-05
- head_second: float32 [8, 2048, 918], P('dp', 'ns'), may hold values from 2.2114943e-13 to 8.7625247e-13
- norm_params: float32 [2, 2, 3072], replicated, may hold values from -1.5 to 2.5
- norm_first: float32 [2, 2, 3072], replicated, may hold values from -4.5776367e-05 to 4.5776367e-05
- norm_second: float32 [2, 2, 3072], replicated, may hold values from 3.5050099e-12 to 1.4186944e-11
Outputs:
- w_pair_new: float32 [2, 2, 2048, 512], P(None, None, 'ns')
- w_spatial_new: float32 [2, 4608, 512], P(None, 'ns')
- mom_pair_new: float32 [2, 2, 2048, 512], P(None, None, 'ns')
- mom_spatial_new: float32 [2, 4608, 512], P(None, 'ns')
- head_table_new: float32 [8, 2048, 918], P('dp', 'ns')
- head_first_new: float32 [8, 2048, 918], P('dp', 'ns')
- head_second_new: float32 [8, 2048, 918], P('dp', 'ns')
- norm_params_new: float32 [2, 2, 3072], replicated
- norm_first_new: float32 [2, 2, 3072], replicated
- norm_second_new: float32 [2, 2, 3072], replicated
- grad_norm: float32 [], replicated
- loss_sum: float32 [], replicated
- weight_total: float32 [], replicated
The draws below stay inside these ranges and needn't reach their ends.
Inputs may be any that keep to these rules, and one draw needn't show every extreme that they name: `game_ids`: in each aligned block of 16 samples of a micro-batch (the samples of one index of dp) no game is named by more than 4 samples; in some block one game is named by exactly 4.
All inputs are finite; a program needn't handle non-finite values.
Results may differ from the reference program's by a relative error of at most 0.015.
Values may be sent and summed in bfloat16 or wider, within the bound.
No kernel may reach another device: no remote copies, remote signals or barrier semaphores. Data moves between devices by JAX's collectives and lax.ppermute only.
A program may use at most 384 MiB of HBM per device.

```python
import math
import jax
import jax.numpy as jnp
import numpy as np
from jax import lax

C = 2048
MID = 512
ACTIONS = 18
ATOMS = 51
GROUPS = 32
SIDE = 11
BLOCKS = 2
MB = 2
NS_ITERS = 2
STEP = 10
S_DEV = 4
PIX = 121
SAMPLES_MB = 128
GAMES = 8
CAP = 4
HOUT = 918
GNW = 3072
NPARAM = 23965696
N_DP = 8
N_NS = 4


def draw_frames(key, part):
    key = jax.random.fold_in(key, 11)
    rise = jnp.arange(C, dtype=jnp.float32) / C
    base = jnp.clip(jax.random.normal(key, (MB, SAMPLES_MB, PIX, C), jnp.float32), -6.0, 6.0)
    scale_row = 0.5 + rise
    return (base * scale_row).astype(jnp.bfloat16)


def draw_groups(key, part):
    key = jax.random.fold_in(key, 13)
    chance = 10 + 80 * jnp.arange(SAMPLES_MB, dtype=jnp.int32) // SAMPLES_MB
    rolls = jax.random.randint(key, (MB, SAMPLES_MB), 0, 100)
    return (rolls < chance[None, :]).astype(jnp.int32)


def draw_norm_params(key, part):
    key = jax.random.fold_in(key, 12)
    key_gain, key_bias = jax.random.split(key)
    rise = jnp.concatenate([jnp.arange(MID, dtype=jnp.float32) / MID, jnp.arange(MID, dtype=jnp.float32) / MID, jnp.arange(C, dtype=jnp.float32) / C])
    noise = 1.0 + 0.1 * jnp.clip(jax.random.normal(key_gain, (BLOCKS, GNW), jnp.float32), -3.0, 3.0)
    gain_rows = (0.5 + rise) * noise
    bias_rows = 0.3 * jnp.clip(jax.random.normal(key_bias, (BLOCKS, GNW), jnp.float32), -5.0, 5.0)
    return jnp.stack([gain_rows, bias_rows], axis=1)


def rising_moment(key, shape, row_count):
    scale = 0.01 * NPARAM ** (-0.5)
    rise = jnp.arange(row_count, dtype=jnp.float32) / row_count
    base = jnp.clip(jax.random.normal(key, shape, jnp.float32), -6.0, 6.0)
    row_scale = 0.5 + rise
    return scale * base * row_scale[:, None]


def draw_mom_pair(key, part):
    key = jax.random.fold_in(key, 14)
    return rising_moment(key, (BLOCKS, 2, C, MID), C)


def draw_mom_spatial(key, part):
    key = jax.random.fold_in(key, 15)
    return rising_moment(key, (BLOCKS, 9 * MID, MID), 9 * MID)


def plant(values, rng, low, top_value):
    shape = values.shape
    spot = [jax.random.randint(jax.random.fold_in(rng, axis), (), 0, shape[axis]) for axis in range(len(shape))]
    values = values.at[tuple(spot)].set(low)
    longest = shape.index(max(shape))
    spot[longest] = (spot[longest] + 1) % shape[longest]
    return values.at[tuple(spot)].set(top_value)


def block_levels(stream_key, shape, cuts, smallest, high):
    def one(dim, shards_of):
        draws = jax.random.uniform(jax.random.fold_in(jax.random.fold_in(stream_key, 6), dim), (shards_of,), jnp.float32, smallest / len(cuts), high / len(cuts))
        return jnp.repeat(jnp.exp(draws), shape[dim] // shards_of).reshape((-1,) + (1,) * (len(shape) - dim - 1))

    level = one(*cuts[0])
    for cut in cuts[1:]:
        level = level * one(*cut)
    return level


def assign_block(key, own, number, rows, amount, top, bound, skew):
    order = jax.random.permutation(key, amount)
    crowded, ordinary = portions_of(amount, rows * top, bound, skew, True), portions_of(amount, rows * top, bound, skew, False)
    places = jnp.arange(amount)

    def named(tallies, turn):
        used = int((tallies > 0).sum())
        fixed = max(1, used // 4)
        moved = fixed + (places - fixed + turn * (used - fixed)) % max(1, amount - fixed)
        return jnp.zeros((amount,), jnp.int32).at[order[jnp.where(places < fixed, places, moved)]].set(jnp.asarray(tallies, jnp.int32))

    tallies = jnp.where(number % 4 == 0, named(crowded, number // 4), named(ordinary, number - number // 4 - 1))
    mixed = jax.random.permutation(jax.random.fold_in(own, 3), amount)
    giver, taker = mixed[0:amount // 2 * 2:2], mixed[1:amount // 2 * 2:2]
    margin = jnp.minimum(tallies[giver] - 1, bound - tallies[taker]) // 2
    margin = jnp.where((giver == order[0]) | (taker == order[0]) | (tallies[taker] == 0), 0, jnp.maximum(margin, 0))
    moved = jax.random.randint(jax.random.fold_in(own, 4), (amount // 2,), 0, 1 << 20) % (margin + 1)
    tallies = tallies.at[giver].add(-moved).at[taker].add(moved)
    members = jnp.searchsorted(jnp.cumsum(tallies), jnp.arange(rows * top), side="right").astype(jnp.int32)
    table = members.reshape(top, rows).T
    table = table[jax.random.permutation(jax.random.fold_in(own, 1), rows)]
    turn = jax.random.randint(jax.random.fold_in(own, 2), (rows, 1), 0, top)
    return jnp.take_along_axis(table, (jnp.arange(top)[None, :] + turn) % top, axis=1)


def portions_of(count, total, limit, slope, full):
    portions = [(1 << 20) // math.isqrt(rank ** slope) + 1 for rank in range(1, count + 1)]
    largest = limit if full else min(limit, max(-(-total // count), total * portions[0] // sum(portions)))
    least = 1 if total - largest >= count - 1 else 0
    given, spare = [largest] + [least] * (count - 1), total - largest - least * (count - 1)
    while spare > 0:
        free = [i for i in range(1, count) if given[i] < largest] or [i for i in range(1, count) if given[i] < limit]
        whole, budget = sum([portions[i] for i in free]), spare
        for i in free:
            addition = min(limit - given[i], max(1, budget * portions[i] // whole), spare)
            given[i] = given[i] + addition
            spare = spare - addition
    return np.array(given)


def gaussian(own_key, dims, width, most, shards=(), kind=jnp.bfloat16):
    array = width * jax.random.normal(own_key, dims, jnp.float32)
    if shards:
        array = array * block_levels(own_key, dims, shards, -0.22, 0.18)
    return jnp.clip(array, -most, most).astype(kind)


def setup_inputs(seed: int = 0) -> dict:
    arg_keys = jax.random.split(jax.random.key(seed), 16)
    frames = draw_frames(jax.random.fold_in(arg_keys[15], 71), 0)
    game_ids_keys = jax.random.split(jax.random.fold_in(arg_keys[1], 1), MB * SAMPLES_MB // (N_NS * S_DEV))
    game_ids_turns = jax.random.permutation(jax.random.fold_in(arg_keys[1], 3), MB * SAMPLES_MB // (N_NS * S_DEV))
    game_ids = jax.vmap(lambda own, number: assign_block(jax.random.fold_in(arg_keys[1], 2), own, number, N_NS * S_DEV, GAMES, 1, CAP, 1))(game_ids_keys, game_ids_turns).reshape((MB, SAMPLES_MB, 1))
    actions = plant(jax.random.randint(arg_keys[2], (MB, SAMPLES_MB), 0, ACTIONS), jax.random.fold_in(arg_keys[2], 1), 0, ACTIONS - 1).astype(jnp.int32)
    groups = draw_groups(jax.random.fold_in(arg_keys[15], 71), 0)
    targets = gaussian(arg_keys[4], (MB, SAMPLES_MB), 0.3, 1.796875, ((1, 32),))
    w_pair = gaussian(arg_keys[5], (BLOCKS, 2, C, MID), C ** -0.5, 0.125, ((2, 4),), jnp.float32)
    w_spatial = gaussian(arg_keys[6], (BLOCKS, 9 * MID, MID), (9 * MID) ** -0.5, 0.09375, ((1, 4),), jnp.float32)
    mom_pair = draw_mom_pair(jax.random.fold_in(arg_keys[15], 71), 0)
    mom_spatial = draw_mom_spatial(jax.random.fold_in(arg_keys[15], 71), 0)
    head_table = gaussian(arg_keys[9], (GAMES, C, HOUT), (C // 8) ** -0.5, 0.375, ((0, 8), (1, 4)), jnp.float32)
    head_first = gaussian(arg_keys[10], (GAMES, C, HOUT), (0.01 * NPARAM ** -0.5), 1.1444091796875e-05, ((0, 8), (1, 4)), jnp.float32)
    head_second = jnp.clip(jnp.exp(math.log(8.762524668533278e-13) - 1.3768156 * jax.random.uniform(arg_keys[11], (GAMES, C, HOUT), jnp.float32) ** block_levels(arg_keys[11], (GAMES, C, HOUT), ((0, 8), (1, 4)), -0.2, 0.2)), 2.2114943340131865e-13, 8.762524668533278e-13)
    norm_params = draw_norm_params(jax.random.fold_in(arg_keys[15], 71), 0)
    norm_first = gaussian(arg_keys[13], (BLOCKS, 2, GNW), (0.04 * NPARAM ** -0.5), 4.57763671875e-05, (), jnp.float32)
    norm_second = jnp.clip(jnp.exp(jax.random.uniform(arg_keys[14], (BLOCKS, 2, GNW), jnp.float32, math.log(3.5050098674133112e-12), math.log(1.4186944154170877e-11))), 3.5050098674133112e-12, 1.4186944154170877e-11)
    return {"frames": frames, "game_ids": game_ids, "actions": actions, "groups": groups, "targets": targets, "w_pair": w_pair, "w_spatial": w_spatial, "mom_pair": mom_pair, "mom_spatial": mom_spatial, "head_table": head_table, "head_first": head_first, "head_second": head_second, "norm_params": norm_params, "norm_first": norm_first, "norm_second": norm_second}


@jax.custom_vjp
def low(v):
    return lax.optimization_barrier(v.astype(jnp.bfloat16)).astype(jnp.float32)

@jax.custom_vjp
def low_back(v):
    return v

def low_keep(v):
    return (low(v), None)

def low_pass(kept, grad):
    return (grad,)

def back_keep(v):
    return (v, None)

def back_low(kept, grad):
    return (low(grad),)
low.defvjp(low_keep, low_pass)
low_back.defvjp(back_keep, back_low)
highest = lax.Precision.HIGHEST
eps_norm = 1e-05
decay_moment = 0.5
beta_second = 0.95
adam_eps = 1e-08
rate_muon = 0.2
decay_muon = 0.01
rate_head = 0.02
decay_head = 0.01
rate_gain = 0.05
clip_limit = 0.01
cql_alpha = 0.05
value_max = 3.0
coef_a = 3.4445
coef_b = -4.775
coef_c = 2.0315

def group_norm(stream, gain, bias):
    frame_count, pixel_count, channels = stream.shape
    grouped = stream.reshape(frame_count, pixel_count, GROUPS, channels // GROUPS)
    center = lax.optimization_barrier(jnp.mean(grouped, axis=(1, 3), keepdims=True))
    spread = lax.optimization_barrier(jnp.mean(jnp.square(grouped - center), axis=(1, 3), keepdims=True))
    normed = ((grouped - center) * lax.rsqrt(spread + eps_norm)).reshape(frame_count, pixel_count, channels)
    return normed * gain + bias

def spread_taps(hidden):
    frame_count, pixel_count, channels = hidden.shape
    grid = hidden.reshape(frame_count, SIDE, SIDE, channels)
    padded = jnp.pad(grid, ((0, 0), (1, 1), (1, 1), (0, 0)))
    pieces = [padded[:, row_off:row_off + SIDE, col_off:col_off + SIDE, :] for row_off in range(3) for col_off in range(3)]
    return jnp.concatenate(pieces, axis=3).reshape(frame_count, pixel_count, 9 * channels)

def gain_parts(gain_rows):
    return (gain_rows[0, :MID], gain_rows[1, :MID], gain_rows[0, MID:2 * MID], gain_rows[1, MID:2 * MID], gain_rows[0, 2 * MID:], gain_rows[1, 2 * MID:])

def sample_loss(logits, sample_meta, support):
    dist = jax.nn.softmax(logits.reshape(-1, ACTIONS, ATOMS), axis=2)
    q_values = lax.optimization_barrier(jnp.sum(dist * support, axis=2))
    action_hot = (sample_meta[:, 3:4] == jnp.arange(ACTIONS, dtype=jnp.float32)[None, :]).astype(jnp.float32)
    chosen = lax.optimization_barrier(jnp.sum(q_values * action_hot, axis=1))
    soft_top = jax.nn.logsumexp(q_values, axis=1)
    return sample_meta[:, 1] * (jnp.square(chosen - sample_meta[:, 0]) + cql_alpha * (soft_top - chosen))

def block_forward(stream, w_first, w_middle, w_last, gain_rows):
    g_one, b_one, g_two, b_two, g_three, b_three = gain_parts(gain_rows)
    first_out = low_back(jnp.einsum('fpc,cm->fpm', low(stream), w_first, precision=highest))
    tap_rows = spread_taps(low(jax.nn.silu(group_norm(first_out, g_one, b_one))))
    middle = low_back(jnp.einsum('fpk,km->fpm', tap_rows, w_middle, precision=highest))
    second = low(jax.nn.silu(group_norm(middle, g_two, b_two)))
    last_out = low_back(jnp.einsum('fpm,cm->fpc', second, w_last, precision=highest))
    return jax.nn.silu(stream + group_norm(last_out, g_three, b_three))

def loss_total(w_pair, w_spatial, head_table, norm_params, stream_in, sample_meta, game_hot):
    pair_low = low(w_pair)
    spatial_low = low(w_spatial)
    head_low = low(head_table)
    support = value_max * (jnp.arange(ATOMS, dtype=jnp.float32) * (2.0 / (ATOMS - 1)) - 1.0)

    def torso(frame_block):
        stream = frame_block
        for layer_idx in range(BLOCKS):
            stream = block_forward(stream, pair_low[layer_idx, 0], spatial_low[layer_idx], pair_low[layer_idx, 1], norm_params[layer_idx])
        return lax.optimization_barrier(jnp.mean(stream, axis=1))
    total_sum = jnp.zeros((), jnp.float32)
    for micro_idx in range(MB):
        blocks_in = stream_in[micro_idx].reshape(N_DP, S_DEV * N_NS, PIX, C)
        pooled = lax.map(jax.checkpoint(torso), blocks_in).reshape(SAMPLES_MB, C)
        sent = low(low_back(pooled))
        per_game = jnp.einsum('sc,gco->sgo', sent, head_low, precision=highest)
        logits = low_back(jnp.einsum('sg,sgo->so', game_hot[micro_idx], per_game, precision=highest))
        total_sum = total_sum + jnp.sum(sample_loss(logits, sample_meta[micro_idx], support))
    return total_sum

def newton_step(current, gram_mat):
    poly_mat = coef_b * gram_mat + coef_c * jnp.einsum('...ij,...jk->...ik', gram_mat, gram_mat, precision=highest)
    return coef_a * current + jnp.einsum('...ri,...ij->...rj', current, poly_mat, precision=highest)

def orthogonal(moment):
    frob_norm = jnp.sqrt(lax.optimization_barrier(jnp.sum(jnp.square(moment), axis=(-2, -1), keepdims=True)))
    current = moment / (frob_norm + 1e-07)
    for sweep_idx in range(NS_ITERS):
        gram_mat = jnp.einsum('...ri,...rj->...ij', current, current, precision=highest)
        current = newton_step(current, gram_mat)
    return current

def adam_step(weight, first, second, grad_in, rate, decay):
    first_new = decay_moment * first + (1.0 - decay_moment) * grad_in
    second_new = beta_second * second + (1.0 - beta_second) * grad_in * grad_in
    normed = first_new / (1.0 - decay_moment ** STEP) / (jnp.sqrt(second_new / (1.0 - beta_second ** STEP)) + adam_eps)
    return (weight - rate * (normed + decay * weight), first_new, second_new)

def reference(frames, game_ids, actions, groups, targets, w_pair, w_spatial, mom_pair, mom_spatial, head_table, head_first, head_second, norm_params, norm_first, norm_second):
    weights = 0.25 + 0.75 * groups.astype(jnp.float32)
    sample_meta = jnp.stack([targets.astype(jnp.float32), weights, game_ids[..., 0].astype(jnp.float32), actions.astype(jnp.float32)], axis=2)
    game_hot = (game_ids[..., 0:1] == jnp.arange(GAMES, dtype=jnp.int32)[None, None, :]).astype(jnp.float32)
    stream_in = frames.astype(jnp.float32)

    def objective(pair_in, spatial_in, head_in, norm_in):
        return loss_total(pair_in, spatial_in, head_in, norm_in, stream_in, sample_meta, game_hot)
    loss_sum, pullback = jax.vjp(objective, w_pair, w_spatial, head_table, norm_params)
    grad_pair, grad_spatial, grad_head, grad_gain = pullback(jnp.ones((), jnp.float32))
    weight_total = jnp.sum(weights)
    square_sum = jnp.sum(jnp.square(grad_pair)) + jnp.sum(jnp.square(grad_spatial)) + jnp.sum(jnp.square(grad_head)) + jnp.sum(jnp.square(grad_gain))
    grad_norm = jnp.sqrt(square_sum) / weight_total
    factor = jnp.minimum(1.0, clip_limit / grad_norm) / weight_total
    pair_moment = decay_moment * mom_pair + factor * grad_pair
    spatial_moment = decay_moment * mom_spatial + factor * grad_spatial
    pair_new = w_pair - rate_muon * (decay_muon * w_pair + 0.2 * math.sqrt(C) * orthogonal(pair_moment))
    spatial_new = w_spatial - rate_muon * (decay_muon * w_spatial + 0.2 * math.sqrt(9 * MID) * orthogonal(spatial_moment))
    head_new, head_first_new, head_second_new = adam_step(head_table, head_first, head_second, factor * grad_head, rate_head, decay_head)
    norm_new, norm_first_new, norm_second_new = adam_step(norm_params, norm_first, norm_second, factor * grad_gain, rate_gain, 0.0)
    return (pair_new, spatial_new, pair_moment, spatial_moment, head_new, head_first_new, head_second_new, norm_new, norm_first_new, norm_second_new, grad_norm, loss_sum, weight_total)
```

```python
import functools
import math

import jax
import jax.numpy as jnp
import numpy as np
from jax import lax
from jax.experimental import pallas as pl
from jax.experimental.pallas import tpu as pltpu
from jax.sharding import PartitionSpec as P

C = 2048
MID = 512
ACTIONS = 18
ATOMS = 51
GROUPS = 32
SIDE = 11
PIX = SIDE * SIDE
BLOCKS = 2
MB = 2
STEP = 10
SEG = 64
HPAD = ACTIONS * SEG
HOUT = ACTIONS * ATOMS

bf16 = jnp.bfloat16
f32 = jnp.float32

eps_norm = 1e-05
decay_moment = 0.5
beta_second = 0.95
adam_eps = 1e-08
rate_muon = 0.2
decay_muon = 0.01
rate_head = 0.02
decay_head = 0.01
rate_gain = 0.05
clip_limit = 0.01
cql_alpha = 0.05
value_max = 3.0
coef_a = 3.4445
coef_b = -4.775
coef_c = 2.0315

FROWS = 128
FPB = 2
BROWS = FPB * FROWS
TAPS = [(dr, dc) for dr in (-1, 0, 1) for dc in (-1, 0, 1)]
MIB = 1024 * 1024


def tap_masks():
    pixel = np.arange(FROWS)
    row, col = pixel // SIDE, pixel % SIDE
    masks = [
        (pixel < PIX) & (row + dr >= 0) & (row + dr < SIDE) & (col + dc >= 0) & (col + dc < SIDE)
        for dr, dc in TAPS
    ]
    return np.repeat(np.stack(masks).astype(np.float32).reshape(9 * FROWS, 1), 128, axis=1)


class Net:
    def __init__(self, dp, ns):
        self.dp, self.ns = dp, ns
        self.ns_bits = [1 << i for i in range(ns.bit_length() - 1)]
        self.dp_bits = [1 << i for i in range(dp.bit_length() - 1)]
        self.plain = not (dp == 8 and ns == 4)

    def swap(self, value, axis, bit):
        pairs = []
        for d in range(self.dp):
            for n in range(self.ns):
                partner = (d ^ bit) * self.ns + n if axis == "dp" else d * self.ns + (n ^ bit)
                pairs.append((d * self.ns + n, partner))
        return lax.ppermute(value, ("dp", "ns"), pairs)

    def add_all(self, value, axes=("dp", "ns")):
        for axis in axes:
            for bit in self.dp_bits if axis == "dp" else self.ns_bits:
                value = value + self.swap(value, axis, bit)
        return value


def pick(value, index, axis):
    return lax.dynamic_index_in_dim(value, index, axis, keepdims=False)


def bit_of(index, shift):
    return lax.rem(lax.div(index, 1 << shift), 2)


class Shards:
    def __init__(self, arrays, offsets):
        self.arrays, self.offsets = arrays, offsets


def gather_rows(net, shards):
    if net.plain:
        return [Shards((lax.all_gather(s.astype(bf16), "ns", axis=0, tiled=True),), None) for s in shards]
    core = bit_of(lax.axis_index("dp"), 0)
    parts, offsets, start = [], [], 0
    for s in shards:
        n = s.shape[0] // 4
        parts.append(pick(s.astype(bf16).reshape(2, 2, n, MID), core, 0))
        offsets.append((start, n))
        start += n
    own = jnp.concatenate(parts, axis=1) if len(parts) > 1 else parts[0]
    path_a, path_b = own[0:1], own[1:2]
    two_a = jnp.concatenate([path_a, net.swap(path_a, "ns", 1)], axis=0)
    two_b = jnp.concatenate([path_b, net.swap(path_b, "ns", 2)], axis=0)
    four_a = net.swap(two_a, "ns", 2)
    four_b = net.swap(two_b, "ns", 1)
    mine = jnp.concatenate([two_a, four_a, two_b, four_b], axis=0)
    other = net.swap(mine, "dp", 1)
    return [Shards((mine, other), off) for off in offsets]


def load_rows(shard, refs, pos_ref, buffer, sems):
    if shard.offsets is None:
        copy = pltpu.make_async_copy(refs[0], buffer, sems.at[0])
        copy.start()
        copy.wait()
        return
    start, n = shard.offsets
    here, core = pos_ref[0], pos_ref[1]
    copies = []
    for half, ref in enumerate(refs):
        for k in range(8):
            path = k // 4
            rel = k if path == 0 else (0, 2, 1, 3)[k - 4]
            place = ((here ^ rel) * 4 + (core ^ half) * 2 + path) * n
            copies.append(
                pltpu.make_async_copy(
                    ref.at[k, pl.ds(start, n)],
                    buffer.at[pl.ds(pl.multiple_of(place, 16), n)],
                    sems.at[half * 8 + k],
                )
            )
    for copy in copies:
        copy.start()
    for copy in copies:
        copy.wait()


def reduce_rows(net, grads):
    if net.plain:
        out = []
        for g in grads:
            share = lax.psum_scatter(g.astype(f32), "ns", scatter_dimension=0, tiled=True)
            out.append(lax.psum(share, "dp").astype(bf16))
        return out
    dp_idx, ns_idx = lax.axis_index("dp"), lax.axis_index("ns")
    core, z_low = bit_of(dp_idx, 0), bit_of(dp_idx, 1)
    x, y = bit_of(ns_idx, 0), bit_of(ns_idx, 1)
    sizes = [g.shape[0] // 16 for g in grads]

    def half(which):
        parts = [
            pick(g.reshape(4, 2, 2, n, MID), which, 1) for g, n in zip(grads, sizes, strict=True)
        ]
        return jnp.concatenate(parts, axis=2) if len(parts) > 1 else parts[0]

    got = net.swap(half(1 - core), "dp", 1)
    total = half(core) + got
    rows = total.shape[2]
    first = total[:, 0].reshape(2, 2, rows, MID)
    second = total[:, 1].reshape(2, 2, rows, MID)
    got_a = net.swap(pick(first, 1 - x, 1), "ns", 1)
    got_b = net.swap(pick(second, 1 - y, 0), "ns", 2)
    first = pick(first, x, 1) + got_a
    second = pick(second, y, 0) + got_b
    got_a = net.swap(pick(first, 1 - y, 0), "ns", 2)
    got_b = net.swap(pick(second, 1 - x, 0), "ns", 1)
    both = jnp.stack([pick(first, y, 0) + got_a, pick(second, x, 0) + got_b])
    kept = pick(both, z_low, 0) + net.swap(pick(both, 1 - z_low, 0), "dp", 2)
    kept = kept + net.swap(kept, "dp", 4)
    given = net.swap(kept, "dp", 2)
    low = z_low == 0
    whole = jnp.stack([jnp.where(low, kept, given), jnp.where(low, given, kept)])
    other = net.swap(whole, "dp", 1)
    lead = core == 0
    whole = jnp.stack([jnp.where(lead, whole, other), jnp.where(lead, other, whole)])
    out, start = [], 0
    for n in sizes:
        out.append(whole[:, :, start : start + n].reshape(4 * n, MID))
        start += n
    return out


GRAM_ROWS = MID + 64


def pack_grams(upper, lower):
    row = lax.broadcasted_iota(jnp.int32, (MID, MID), 0)
    col = lax.broadcasted_iota(jnp.int32, (MID, MID), 1)
    body = jnp.where(row < col, upper, lower)
    diag = jnp.sum(jnp.where(row == col, upper, 0.0), axis=-2, keepdims=True)
    tail = jnp.broadcast_to(diag, diag.shape[:-2] + (GRAM_ROWS - MID, MID))
    return jnp.concatenate([body, tail], axis=-2).astype(bf16)


def unpack_grams(packed):
    packed = packed.astype(f32)
    body, diag = packed[..., :MID, :], packed[..., MID : MID + 1, :]
    row = lax.broadcasted_iota(jnp.int32, (MID, MID), 0)
    col = lax.broadcasted_iota(jnp.int32, (MID, MID), 1)
    flip = jnp.swapaxes(body, -1, -2)
    upper = jnp.where(row < col, body, jnp.where(row == col, diag, flip))
    lower = jnp.where(row < col, flip, body)
    return upper, lower


def reduce_grams(net, packed):
    if net.plain:
        return lax.psum(packed.astype(f32), "ns").astype(bf16)
    n = packed.shape[0]
    core = bit_of(lax.axis_index("dp"), 0)
    mine = pick(packed.reshape(n, 2, 2, GRAM_ROWS // 4, MID), core, 1)
    first, second = mine[:, 0], mine[:, 1]
    first, second = first + net.swap(first, "ns", 1), second + net.swap(second, "ns", 2)
    first, second = first + net.swap(first, "ns", 2), second + net.swap(second, "ns", 1)
    mine = jnp.stack([first, second], axis=1)
    other = net.swap(mine, "dp", 1)
    lead = core == 0
    whole = jnp.stack([jnp.where(lead, mine, other), jnp.where(lead, other, mine)], axis=1)
    return whole.reshape(n, GRAM_ROWS, MID)


def sigmoid(v):
    return 0.5 * jnp.tanh(0.5 * v) + 0.5


def group_sum(t, size):
    tiles = t.shape[1] // 128
    u = jnp.concatenate([t[:, j * 128 : (j + 1) * 128] for j in range(tiles)], axis=0)
    lane = lax.broadcasted_iota(jnp.int32, u.shape, 1)
    step = 1
    while step < size:
        u = u + jnp.where(
            (lane & step) == 0, pltpu.roll(u, 128 - step, 1), pltpu.roll(u, step, 1)
        )
        step *= 2
    return jnp.concatenate([u[8 * j : 8 * j + 8] for j in range(tiles)], axis=1)


def live_rows():
    return lax.broadcasted_iota(jnp.int32, (FROWS, 128), 0) < PIX


def norm_stats(st, size):
    sums = group_sum(st[...], size) * (1.0 / (PIX * size))
    mean = sums[0:FPB]
    spread = jnp.maximum(sums[FPB : 2 * FPB] - mean * mean, 0.0)
    return mean, lax.rsqrt(spread + eps_norm)


def add_stats(st, f, lanes, v):
    st[f : f + 1, lanes] = jnp.sum(v, axis=0, keepdims=True)
    st[FPB + f : FPB + f + 1, lanes] = jnp.sum(v * v, axis=0, keepdims=True)


def units(width):
    for j in range(width // 128):
        for f in range(FPB):
            yield f, pl.ds(f * FROWS, FROWS), slice(j * 128, (j + 1) * 128)


def first_step(body):
    pl.when(pl.program_id(0) == 0)(body)


def reduce_kernel(shard, pos, x, gb, *rest):
    n = len(shard.arrays)
    refs, (h, xh, rs, buf, sems, acc, st) = rest[:n], rest[n:]

    @first_step
    def _():
        load_rows(shard, refs, pos, buf, sems)
        st[...] = jnp.zeros_like(st)

    for j in range(MID // 256):
        lanes = slice(j * 256, (j + 1) * 256)
        a = jnp.dot(x[...], buf[:, lanes], preferred_element_type=f32)
        acc[:, lanes] = a
        for f in range(FPB):
            add_stats(st, f, lanes, a[f * FROWS : (f + 1) * FROWS])
    norm_out(acc, st, gb, h, xh, rs)


def norm_out(acc, st, gb, h, xh, rs):
    mean, rstd = norm_stats(st, MID // GROUPS)
    rs[...] = jnp.zeros_like(rs)
    rs[0:FPB] = rstd
    live = live_rows()
    for f, rows, lanes in units(MID):
        v = jnp.where(live, (acc[rows, lanes] - mean[f : f + 1, lanes]) * rstd[f : f + 1, lanes], 0.0)
        xh[rows, lanes] = v.astype(bf16)
        v = v * gb[0:1, lanes] + gb[1:2, lanes]
        h[rows, lanes] = jnp.where(live, v * sigmoid(v), 0.0).astype(bf16)


def spread_taps(src, masks, taps):
    for f, rows, lanes in units(MID):
        v = src[rows, lanes].astype(f32)
        for k, (dr, dc) in enumerate(TAPS):
            shift = -(dr * SIDE + dc)
            t = v if shift == 0 else pltpu.roll(v, shift % FROWS, 0)
            t = t * masks[k * FROWS : (k + 1) * FROWS]
            taps[rows, k * MID + lanes.start : k * MID + lanes.stop] = t.astype(bf16)


def conv_kernel(shard, pos, src, masks, gb, *rest):
    n = len(shard.arrays)
    refs, (taps, u2, xh, rs, buf, sems, acc, st) = rest[:n], rest[n:]

    @first_step
    def _():
        load_rows(shard, refs, pos, buf, sems)
        st[...] = jnp.zeros_like(st)

    spread_taps(src, masks, taps)
    for j in range(MID // 256):
        lanes = slice(j * 256, (j + 1) * 256)
        a = jnp.dot(taps[...], buf[:, lanes], preferred_element_type=f32)
        acc[:, lanes] = a
        for f in range(FPB):
            add_stats(st, f, lanes, a[f * FROWS : (f + 1) * FROWS])
    norm_out(acc, st, gb, u2, xh, rs)


def expand_kernel(shard, last, pos, u2, x, gb, *rest):
    n = len(shard.arrays)
    refs, (xh, rs, out, buf, sems, acc, st) = rest[:n], rest[n:]

    @first_step
    def _():
        load_rows(shard, refs, pos, buf, sems)
        st[...] = jnp.zeros_like(st)

    for j in range(C // 256):
        lanes = slice(j * 256, (j + 1) * 256)
        a = lax.dot_general(
            u2[...], buf[lanes, :], (((1,), (1,)), ((), ())), preferred_element_type=f32
        )
        acc[:, lanes] = a
        for f in range(FPB):
            add_stats(st, f, lanes, a[f * FROWS : (f + 1) * FROWS])
    mean, rstd = norm_stats(st, C // GROUPS)
    rs[...] = jnp.zeros_like(rs)
    rs[0:FPB] = rstd
    if last:
        out[...] = jnp.zeros_like(out)
    live = live_rows()
    for f, rows, lanes in units(C):
        v = jnp.where(live, (acc[rows, lanes] - mean[f : f + 1, lanes]) * rstd[f : f + 1, lanes], 0.0)
        xh[rows, lanes] = v.astype(bf16)
        v = x[rows, lanes].astype(f32) + (v * gb[0:1, lanes] + gb[1:2, lanes])
        v = jnp.where(live, v * sigmoid(v), 0.0)
        if last:
            out[f : f + 1, lanes] = jnp.sum(v, axis=0, keepdims=True) * (1.0 / PIX)
        else:
            out[rows, lanes] = v.astype(bf16)


def back_sums(st, f, lanes, dv, xhat, gain, gacc):
    by_gain = jnp.sum(dv * xhat, axis=0, keepdims=True)
    by_bias = jnp.sum(dv, axis=0, keepdims=True)
    st[f : f + 1, lanes] = by_bias * gain
    st[FPB + f : FPB + f + 1, lanes] = by_gain * gain
    gacc[0:1, lanes] += by_gain
    gacc[1:2, lanes] += by_bias


def back_norm(st, size):
    sums = group_sum(st[...], size) * (1.0 / (PIX * size))
    return sums[0:FPB], sums[FPB : 2 * FPB]


def act_back(acc, st, xh, rs, gb, gacc, out):
    live = live_rows()
    for f, rows, lanes in units(MID):
        xhat = xh[rows, lanes].astype(f32)
        v = xhat * gb[0:1, lanes] + gb[1:2, lanes]
        s = sigmoid(v)
        dv = jnp.where(live, acc[rows, lanes] * (s + v * s * (1.0 - s)), 0.0)
        acc[rows, lanes] = dv
        back_sums(st, f, lanes, dv, xhat, gb[0:1, lanes], gacc)
    m1, m2 = back_norm(st, MID // GROUPS)
    for f, rows, lanes in units(MID):
        xhat = xh[rows, lanes].astype(f32)
        da = rs[f : f + 1, lanes] * (
            acc[rows, lanes] * gb[0:1, lanes] - m1[f : f + 1, lanes] - xhat * m2[f : f + 1, lanes]
        )
        out[rows, lanes] = jnp.where(live, da, 0.0).astype(bf16)


def tail_back_kernel(shard, last, pos, d, x, xh3, rs3, gb3, xh2, rs2, gb2, *rest):
    n = len(shard.arrays)
    refs, (r, da3, da2, gacc3, gacc2, buf, sems, acc, st, acc2, st2) = rest[:n], rest[n:]

    @first_step
    def _():
        load_rows(shard, refs, pos, buf, sems)
        st[...] = jnp.zeros_like(st)
        st2[...] = jnp.zeros_like(st2)
        gacc3[...] = jnp.zeros_like(gacc3)
        gacc2[...] = jnp.zeros_like(gacc2)

    live = live_rows()
    for f, rows, lanes in units(C):
        xhat = xh3[rows, lanes].astype(f32)
        v = x[rows, lanes].astype(f32) + (xhat * gb3[0:1, lanes] + gb3[1:2, lanes])
        s = sigmoid(v)
        grad = d[f : f + 1, lanes] if last else d[rows, lanes].astype(f32)
        dv = jnp.where(live, grad * (s + v * s * (1.0 - s)), 0.0)
        acc[rows, lanes] = dv
        r[rows, lanes] = dv.astype(bf16)
        back_sums(st, f, lanes, dv, xhat, gb3[0:1, lanes], gacc3)
    m1, m2 = back_norm(st, C // GROUPS)
    for f, rows, lanes in units(C):
        xhat = xh3[rows, lanes].astype(f32)
        da = rs3[f : f + 1, lanes] * (
            acc[rows, lanes] * gb3[0:1, lanes] - m1[f : f + 1, lanes] - xhat * m2[f : f + 1, lanes]
        )
        da3[rows, lanes] = jnp.where(live, da, 0.0).astype(bf16)
    for j in range(MID // 256):
        lanes = slice(j * 256, (j + 1) * 256)
        acc2[:, lanes] = jnp.dot(da3[...], buf[:, lanes], preferred_element_type=f32)
    act_back(acc2, st2, xh2, rs2, gb2, gacc2, da2)


def conv_back_kernel(shard, shard_one, pos, da2, masks, xh1, rs1, gb1, *rest):
    n = len(shard.arrays)
    refs, rest = rest[:n], rest[n:]
    if shard_one is not None:
        n = len(shard_one.arrays)
        refs_one, (r, da1, gacc1, d, buf, sems, taps, acc, st, buf_one, sems_one) = rest[:n], rest[n:]
    else:
        da1, gacc1, buf, sems, taps, acc, st = rest

    @first_step
    def _():
        load_rows(shard, refs, pos, buf, sems)
        if shard_one is not None:
            load_rows(shard_one, refs_one, pos, buf_one, sems_one)
        st[...] = jnp.zeros_like(st)
        gacc1[...] = jnp.zeros_like(gacc1)

    spread_taps(da2, masks, taps)
    for j in range(MID // 256):
        total = None
        for k in range(9):
            part = lax.dot_general(
                taps[:, (8 - k) * MID : (9 - k) * MID],
                buf[k * MID + j * 256 : k * MID + (j + 1) * 256, :],
                (((1,), (1,)), ((), ())),
                preferred_element_type=f32,
            )
            total = part if total is None else total + part
        acc[:, j * 256 : (j + 1) * 256] = total
    act_back(acc, st, xh1, rs1, gb1, gacc1, da1)
    if shard_one is not None:
        for j in range(C // 256):
            lanes = slice(j * 256, (j + 1) * 256)
            a = lax.dot_general(
                da1[...], buf_one[lanes, :], (((1,), (1,)), ((), ())), preferred_element_type=f32
            )
            d[:, lanes] = (r[:, lanes].astype(f32) + a).astype(bf16)


def rows_spec(width):
    return pl.BlockSpec((BROWS, width), lambda i: (i, 0))


def eight_spec(width):
    return pl.BlockSpec((8, width), lambda i: (i, 0))


def whole_spec(rows, width):
    return pl.BlockSpec((rows, width), lambda i: (0, 0))


ANY = pl.BlockSpec(memory_space=pl.ANY)
SMEM = pl.BlockSpec(memory_space=pltpu.SMEM)


def sds(rows, width, dtype):
    return jax.ShapeDtypeStruct((rows, width), dtype)


def call(kernel, name, rows, in_specs, outs, scratch, flops, bytes_accessed, limit=48):
    return pl.pallas_call(
        kernel,
        name=name,
        grid=(rows // BROWS,),
        in_specs=in_specs,
        out_specs=[spec for _, spec in outs],
        out_shape=[shape for shape, _ in outs],
        scratch_shapes=scratch,
        cost_estimate=pl.CostEstimate(
            flops=int(flops), bytes_accessed=int(bytes_accessed), transcendentals=0
        ),
        compiler_params=pltpu.CompilerParams(
            vmem_limit_bytes=limit * MIB, dimension_semantics=("arbitrary",)
        ),
    )


def sem16():
    return pltpu.SemaphoreType.DMA((16,))


def run_reduce(pos, x, shard, gb):
    rows = x.shape[0]
    eights = rows // BROWS * 8
    return call(
        functools.partial(reduce_kernel, shard),
        "reduce_norm",
        rows,
        [SMEM, rows_spec(C), whole_spec(2, MID)] + [ANY] * len(shard.arrays),
        [
            (sds(rows, MID, bf16), rows_spec(MID)),
            (sds(rows, MID, bf16), rows_spec(MID)),
            (sds(eights, MID, f32), eight_spec(MID)),
        ],
        [
            pltpu.VMEM((C, MID), bf16),
            sem16(),
            pltpu.VMEM((BROWS, MID), f32),
            pltpu.VMEM((8, MID), f32),
        ],
        2 * rows * C * MID,
        rows * (C + 2 * MID) * 2 + C * MID * 2,
    )(pos, x, gb, *shard.arrays)


def run_conv(pos, h, masks, shard, gb):
    rows = h.shape[0]
    eights = rows // BROWS * 8
    return call(
        functools.partial(conv_kernel, shard),
        "conv_norm",
        rows,
        [SMEM, rows_spec(MID), whole_spec(9 * FROWS, 128), whole_spec(2, MID)]
        + [ANY] * len(shard.arrays),
        [
            (sds(rows, 9 * MID, bf16), rows_spec(9 * MID)),
            (sds(rows, MID, bf16), rows_spec(MID)),
            (sds(rows, MID, bf16), rows_spec(MID)),
            (sds(eights, MID, f32), eight_spec(MID)),
        ],
        [
            pltpu.VMEM((9 * MID, MID), bf16),
            sem16(),
            pltpu.VMEM((BROWS, MID), f32),
            pltpu.VMEM((8, MID), f32),
        ],
        2 * rows * 9 * MID * MID,
        rows * 12 * MID * 2 + 9 * MID * MID * 2,
    )(pos, h, masks, gb, *shard.arrays)


def run_expand(pos, u2, x, shard, gb, last):
    rows = x.shape[0]
    eights = rows // BROWS * 8
    return call(
        functools.partial(expand_kernel, shard, last),
        "expand_norm",
        rows,
        [SMEM, rows_spec(MID), rows_spec(C), whole_spec(2, C)] + [ANY] * len(shard.arrays),
        [
            (sds(rows, C, bf16), rows_spec(C)),
            (sds(eights, C, f32), eight_spec(C)),
            (sds(eights, C, f32), eight_spec(C)) if last else (sds(rows, C, bf16), rows_spec(C)),
        ],
        [
            pltpu.VMEM((C, MID), bf16),
            sem16(),
            pltpu.VMEM((BROWS, C), f32),
            pltpu.VMEM((8, C), f32),
        ],
        2 * rows * C * MID,
        rows * (3 * C + MID) * 2 + C * MID * 2,
    )(pos, u2, x, gb, *shard.arrays)


def run_tail_back(pos, d, x, xh3, rs3, gb3, xh2, rs2, gb2, shard, last):
    rows = x.shape[0]
    return call(
        functools.partial(tail_back_kernel, shard, last),
        "tail_back",
        rows,
        [
            SMEM,
            eight_spec(C) if last else rows_spec(C),
            rows_spec(C),
            rows_spec(C),
            eight_spec(C),
            whole_spec(2, C),
            rows_spec(MID),
            eight_spec(MID),
            whole_spec(2, MID),
        ]
        + [ANY] * len(shard.arrays),
        [
            (sds(rows, C, bf16), rows_spec(C)),
            (sds(rows, C, bf16), rows_spec(C)),
            (sds(rows, MID, bf16), rows_spec(MID)),
            (sds(8, C, f32), whole_spec(8, C)),
            (sds(8, MID, f32), whole_spec(8, MID)),
        ],
        [
            pltpu.VMEM((C, MID), bf16),
            sem16(),
            pltpu.VMEM((BROWS, C), f32),
            pltpu.VMEM((8, C), f32),
            pltpu.VMEM((BROWS, MID), f32),
            pltpu.VMEM((8, MID), f32),
        ],
        2 * rows * C * MID,
        rows * (5 * C + 2 * MID) * 2 + C * MID * 2,
    )(pos, d, x, xh3, rs3, gb3, xh2, rs2, gb2, *shard.arrays)


def run_conv_back(pos, da2, masks, xh1, rs1, gb1, shard, shard_one, r):
    rows = da2.shape[0]
    more = shard_one is not None
    extra = shard_one.arrays if more else ()
    return call(
        functools.partial(conv_back_kernel, shard, shard_one),
        "conv_back",
        rows,
        [
            SMEM,
            rows_spec(MID),
            whole_spec(9 * FROWS, 128),
            rows_spec(MID),
            eight_spec(MID),
            whole_spec(2, MID),
        ]
        + [ANY] * (len(shard.arrays) + len(extra))
        + ([rows_spec(C)] if more else []),
        [
            (sds(rows, MID, bf16), rows_spec(MID)),
            (sds(8, MID, f32), whole_spec(8, MID)),
        ]
        + ([(sds(rows, C, bf16), rows_spec(C))] if more else []),
        [
            pltpu.VMEM((9 * MID, MID), bf16),
            sem16(),
            pltpu.VMEM((BROWS, 9 * MID), bf16),
            pltpu.VMEM((BROWS, MID), f32),
            pltpu.VMEM((8, MID), f32),
        ]
        + ([pltpu.VMEM((C, MID), bf16), sem16()] if more else []),
        2 * rows * 9 * MID * MID + (2 * rows * C * MID if more else 0),
        rows * 4 * MID * 2 + 9 * MID * MID * 2 + (rows * C * 4 if more else 0),
    )(pos, da2, masks, xh1, rs1, gb1, *shard.arrays, *extra, *([r] if more else []))


def head_in_kernel(select, feats, head, rows_out, logits):
    rows = jnp.dot(select[...], feats[...], preferred_element_type=f32).astype(bf16)
    rows_out[...] = rows
    logits[...] = jnp.dot(rows, head[...], preferred_element_type=f32)


def head_loss_kernel(logits, meta, head, select, grad_out, back, loss, probs):
    count = logits.shape[0]
    lane = lax.broadcasted_iota(jnp.int32, (count, 128), 1)
    spot = lane & (SEG - 1)
    level = value_max * (spot.astype(f32) * (2.0 / (ATOMS - 1)) - 1.0)
    values = jnp.zeros((count, 128), f32)
    columns = []
    for a in range(ACTIONS):
        chunk = slice(a // 2 * 128, a // 2 * 128 + 128)
        inside = (lane >= (a % 2) * SEG) & (lane < (a % 2) * SEG + ATOMS)
        v = logits[:, chunk]
        top = jnp.max(jnp.where(inside, v, -3.0e38), axis=1, keepdims=True)
        e = jnp.where(inside, jnp.exp(jnp.minimum(v - top, 0.0)), 0.0)
        p = e / jnp.sum(e, axis=1, keepdims=True)
        q = jnp.sum(p * level, axis=1, keepdims=True)
        columns.append(q)
        values = jnp.where(lane == a, q, values)
        if a % 2 == 0:
            probs[:, chunk] = p
        else:
            probs[:, chunk] += p
    target, weight, action = meta[:, 0:1], meta[:, 1:2], meta[:, 3:4]
    real = lane < ACTIONS
    hot = (lane.astype(f32) == action).astype(f32)
    chosen = jnp.sum(values * hot, axis=1, keepdims=True)
    top = jnp.max(jnp.where(real, values, -3.0e38), axis=1, keepdims=True)
    e = jnp.where(real, jnp.exp(jnp.minimum(values - top, 0.0)), 0.0)
    total = jnp.sum(e, axis=1, keepdims=True)
    soft_top = top + jnp.log(total)
    row_loss = weight * ((chosen - target) * (chosen - target) + cql_alpha * (soft_top - chosen))
    loss[...] = jnp.zeros(loss.shape, f32) + jnp.sum(row_loss, axis=0, keepdims=True)
    slope = weight * (2.0 * (chosen - target) * hot + cql_alpha * (e / total - hot))
    for j in range(ACTIONS // 2):
        chunk = slice(j * 128, j * 128 + 128)
        low = lane < SEG
        q = jnp.where(low, columns[2 * j], columns[2 * j + 1])
        s = jnp.where(low, slope[:, 2 * j : 2 * j + 1], slope[:, 2 * j + 1 : 2 * j + 2])
        grad_out[:, chunk] = (s * probs[:, chunk] * (level - q)).astype(bf16)
    feat = lax.dot_general(
        grad_out[...], head[...], (((1,), (1,)), ((), ())), preferred_element_type=f32
    ).astype(bf16)
    back[...] = lax.dot_general(
        select[...], feat, (((0,), (0,)), ((), ())), preferred_element_type=f32
    ).astype(bf16)


def plain_call(kernel, name, outs, scratch, limit=48):
    return pl.pallas_call(
        kernel,
        name=name,
        out_shape=outs,
        scratch_shapes=scratch,
        compiler_params=pltpu.CompilerParams(vmem_limit_bytes=limit * MIB),
    )


def adam_step(weight, first, second, grad_in, rate, decay):
    first_new = decay_moment * first + (1.0 - decay_moment) * grad_in
    second_new = beta_second * second + (1.0 - beta_second) * grad_in * grad_in
    normed = (
        first_new
        / (1.0 - decay_moment**STEP)
        / (jnp.sqrt(second_new / (1.0 - beta_second**STEP)) + adam_eps)
    )
    return (weight - rate * (normed + decay * weight), first_new, second_new)


def mat(a, b):
    return jnp.einsum(
        "bij,bjk->bik", a.astype(bf16), b.astype(bf16), preferred_element_type=f32
    )


def gram(a, b):
    return jnp.einsum("ri,rj->ij", a, b, preferred_element_type=f32)


def weight_grad(a, b):
    return jnp.einsum("ri,rj->ij", a, b, preferred_element_type=f32).astype(bf16)


def local(
    net,
    frames,
    game_ids,
    actions,
    groups,
    targets,
    w_pair,
    w_spatial,
    mom_pair,
    mom_spatial,
    head_table,
    head_first,
    head_second,
    norm_params,
    norm_first,
    norm_second,
):
    dp_idx, ns_idx = lax.axis_index("dp"), lax.axis_index("ns")
    pos = jnp.stack([ns_idx, bit_of(dp_idx, 0)]).astype(jnp.int32)
    dev_rows = frames.shape[1]
    samples = MB * dev_rows
    rows = samples * FROWS
    devices = net.dp * net.ns
    everyone = devices * samples
    slots = MB * net.dp * (2 * net.ns * dev_rows // net.dp)
    col_width = C // net.ns

    (w_one0,) = gather_rows(net, [w_pair[0, 0]])
    (w_mid0,) = gather_rows(net, [w_spatial[0]])
    w_last0, w_one1 = gather_rows(net, [w_pair[0, 1], w_pair[1, 0]])
    (w_mid1,) = gather_rows(net, [w_spatial[1]])
    (w_last1,) = gather_rows(net, [w_pair[1, 1]])
    ones, mids, lasts = [w_one0, w_one1], [w_mid0, w_mid1], [w_last0, w_last1]

    meta = jnp.stack(
        [
            targets.astype(f32),
            0.25 + 0.75 * groups.astype(f32),
            game_ids[:, :, 0].astype(f32),
            actions.astype(f32),
        ]
    ).reshape(4, samples)
    meta = jnp.concatenate([meta, jnp.zeros((12, samples), f32)], axis=0).astype(bf16)
    mine = dp_idx * net.ns + ns_idx
    spread = (
        jnp.arange(everyone, dtype=jnp.int32)[None, :]
        == (mine * samples + jnp.arange(samples, dtype=jnp.int32))[:, None]
    ).astype(bf16)
    meta = jnp.dot(meta, spread, preferred_element_type=f32).astype(bf16)
    meta = net.add_all(meta).astype(f32)
    weight_total = jnp.sum(meta[1])
    match = (meta[2].astype(jnp.int32) == dp_idx).astype(jnp.int32)
    place = jnp.cumsum(match) - 1
    select = (
        (jnp.arange(slots, dtype=jnp.int32)[:, None] == place[None, :]) & (match[None, :] == 1)
    ).astype(bf16)
    meta_slots = jnp.einsum("se,me->sm", select, meta.astype(bf16), preferred_element_type=f32)

    out_col = jnp.arange(HOUT, dtype=jnp.int32)
    widen = (
        (out_col // ATOMS * SEG + out_col % ATOMS)[:, None] == jnp.arange(HPAD, dtype=jnp.int32)
    ).astype(bf16)
    head = jnp.dot(head_table[0].astype(bf16), widen, preferred_element_type=f32).astype(bf16)

    moms = [mom_pair[0, 0], mom_pair[0, 1], mom_pair[1, 0], mom_pair[1, 1], mom_spatial[0], mom_spatial[1]]
    moms_low = [m.astype(bf16) for m in moms]
    old = jnp.stack([gram(m, m) for m in moms_low])
    old_sum = reduce_grams(net, pack_grams(old[:3], old[3:]))
    old_upper, old_lower = unpack_grams(old_sum)
    gram_mm = jnp.concatenate([old_upper, old_lower], axis=0)

    masks = jnp.asarray(tap_masks())
    stream = jnp.pad(
        frames.reshape(samples, PIX, C), ((0, 0), (0, FROWS - PIX), (0, 0))
    ).reshape(rows, C)
    gbs = [
        (p[:, :MID], p[:, MID : 2 * MID], p[:, 2 * MID :])
        for p in (norm_params[layer] for layer in range(BLOCKS))
    ]
    kept = []
    for layer in range(BLOCKS):
        gb1, gb2, gb3 = gbs[layer]
        h, xh1, rs1 = run_reduce(pos, stream, ones[layer], gb1)
        taps, u2, xh2, rs2 = run_conv(pos, h, masks, mids[layer], gb2)
        last = layer == BLOCKS - 1
        xh3, rs3, out = run_expand(pos, u2, stream, lasts[layer], gb3, last)
        kept.append((stream, xh1, rs1, taps, u2, xh2, rs2, xh3, rs3))
        stream = out
    pooled = stream.reshape(-1, 8, C)[:, :FPB].reshape(samples, C).astype(bf16)

    sent = jnp.swapaxes(pooled.reshape(samples, net.ns, col_width), 0, 1)
    sent = jnp.broadcast_to(sent[None], (net.dp, net.ns, samples, col_width))
    feats = lax.all_to_all(
        sent.reshape(devices, samples, col_width), ("dp", "ns"), 0, 0, tiled=True
    ).reshape(everyone, col_width)
    feat_rows, logits = plain_call(
        head_in_kernel,
        "head_in",
        [sds(slots, col_width, bf16), sds(slots, HPAD, f32)],
        [],
    )(select, feats, head)
    logits = net.add_all(logits, ("ns",))
    grad_low, back, loss = plain_call(
        head_loss_kernel,
        "head_loss",
        [sds(slots, HPAD, bf16), sds(everyone, col_width, bf16), sds(8, 128, f32)],
        [pltpu.VMEM((slots, HPAD), f32)],
    )(logits, meta_slots, head, select)
    returned = lax.all_to_all(
        back.reshape(devices, samples, col_width), ("dp", "ns"), 0, 0, tiled=True
    ).reshape(net.dp, net.ns, samples, col_width)
    grad_pooled = jnp.sum(returned.astype(f32), axis=0)
    grad_pooled = jnp.swapaxes(grad_pooled, 0, 1).reshape(samples // FPB, FPB, C) * (1.0 / PIX)
    grad_stream = jnp.pad(grad_pooled, ((0, 0), (0, 8 - FPB), (0, 0))).reshape(-1, C)

    grad_low = lax.dot_general(
        grad_low, widen, (((1,), (1,)), ((), ())), preferred_element_type=f32
    ).astype(bf16)
    head_grad = gram(feat_rows, grad_low)
    head_sq = jnp.sum(jnp.square(head_grad))
    loss_part = jnp.where(ns_idx == 0, loss[0, 0], 0.0)

    gain_rows = [None] * BLOCKS
    grads = [None] * BLOCKS
    for layer in reversed(range(BLOCKS)):
        x, xh1, rs1, taps, u2, xh2, rs2, xh3, rs3 = kept[layer]
        gb1, gb2, gb3 = gbs[layer]
        r, da3, da2, gacc3, gacc2 = run_tail_back(
            pos, grad_stream, x, xh3, rs3, gb3, xh2, rs2, gb2, lasts[layer], layer == BLOCKS - 1
        )
        grad_last = weight_grad(da3, u2)
        grad_mid = weight_grad(taps, da2)
        got = run_conv_back(
            pos, da2, masks, xh1, rs1, gb1, mids[layer], ones[layer] if layer > 0 else None, r
        )
        da1, gacc1 = got[:2]
        grad_one = weight_grad(x, da1)
        if layer > 0:
            grad_stream = got[2]
        grads[layer] = (grad_one, grad_last, grad_mid)
        gain_rows[layer] = jnp.concatenate([gacc1[:2], gacc2[:2], gacc3[:2]], axis=1)

    shares = [None] * 6
    shares[2], shares[3], shares[5] = reduce_rows(net, list(grads[1]))
    shares[1], shares[4] = reduce_rows(net, [grads[0][1], grads[0][2]])
    (shares[0],) = reduce_rows(net, [grads[0][0]])

    def cross_grams(ids):
        packs = []
        for i in ids:
            s = gram(moms_low[i], shares[i])
            packs.append(pack_grams(s + s.T, gram(shares[i], shares[i])))
        return unpack_grams(reduce_grams(net, jnp.stack(packs)))

    mg_b, gg_b = cross_grams([2, 3, 5])
    mg_m, gg_m = cross_grams([1, 4])
    mg_a, gg_a = cross_grams([0])
    gram_mg = jnp.stack([mg_a[0], mg_m[0], mg_b[0], mg_b[1], mg_m[1], mg_b[2]])
    gram_gg = jnp.stack([gg_a[0], gg_m[0], gg_b[0], gg_b[1], gg_m[1], gg_b[2]])

    small = jnp.stack(gain_rows).reshape(-1, 1024)
    tail = jnp.zeros((16 - small.shape[0], 1024), f32)
    lane = jnp.arange(1024, dtype=jnp.int32)[None, :]
    tail = tail + jnp.where(lane == 0, loss_part, 0.0) + jnp.where(lane == 1, head_sq, 0.0)
    small = net.add_all(jnp.concatenate([small, tail], axis=0))
    gain_sum = small[:12].reshape(BLOCKS, 2, 2 * MID + C)
    loss_sum, head_total = small[12, 0], small[12, 1]

    eye = jnp.eye(MID, dtype=f32)
    diag_gg = jnp.sum(gram_gg * eye)
    grad_norm = jnp.sqrt(diag_gg + head_total + jnp.sum(jnp.square(gain_sum))) / weight_total
    factor = jnp.minimum(1.0, clip_limit / grad_norm) / weight_total

    gram_all = (
        decay_moment * decay_moment * gram_mm
        + (decay_moment * factor) * gram_mg
        + (factor * factor) * gram_gg
    )
    frob = jnp.sqrt(jnp.maximum(jnp.sum(gram_all * eye, axis=(1, 2)), 0.0))
    scale = 1.0 / (frob + 1e-07)
    g0 = gram_all * (scale * scale)[:, None, None]
    e1 = coef_b * g0 + coef_c * mat(g0, g0)
    k = coef_a * g0 + mat(g0, e1)
    g1 = coef_a * k + mat(k, e1)
    e2 = coef_b * g1 + coef_c * mat(g1, g1)
    poly = coef_a * (e1 + e2) + mat(e1, e2)

    news, moments = [], []
    weights = [w_pair[0, 0], w_pair[0, 1], w_pair[1, 0], w_pair[1, 1], w_spatial[0], w_spatial[1]]
    for i in range(6):
        moment = decay_moment * moms[i] + factor * shares[i].astype(f32)
        current = moment * scale[i]
        ortho = (coef_a * coef_a) * current + jnp.dot(
            current.astype(bf16), poly[i].astype(bf16), preferred_element_type=f32
        )
        gain = 0.2 * math.sqrt(C if i < 4 else 9 * MID)
        news.append(weights[i] - rate_muon * (decay_muon * weights[i] + gain * ortho))
        moments.append(moment)

    head_new, head_first_new, head_second_new = adam_step(
        head_table, head_first, head_second, factor * head_grad[None], rate_head, decay_head
    )
    norm_new, norm_first_new, norm_second_new = adam_step(
        norm_params, norm_first, norm_second, factor * gain_sum, rate_gain, 0.0
    )

    def pair(v):
        return jnp.stack([jnp.stack(v[0:2]), jnp.stack(v[2:4])])

    return (
        pair(news),
        jnp.stack(news[4:]),
        pair(moments),
        jnp.stack(moments[4:]),
        head_new,
        head_first_new,
        head_second_new,
        norm_new,
        norm_first_new,
        norm_second_new,
        grad_norm,
        loss_sum,
        weight_total,
    )


def solution(mesh):
    net = Net(mesh.shape["dp"], mesh.shape["ns"])
    samples = P(None, ("dp", "ns"))
    heads = P("dp", "ns", None)
    pairs, spatial = P(None, None, "ns", None), P(None, "ns", None)
    in_specs = (
        P(None, ("dp", "ns"), None, None),
        P(None, ("dp", "ns"), None),
        samples,
        samples,
        samples,
        pairs,
        spatial,
        pairs,
        spatial,
        heads,
        heads,
        heads,
        P(),
        P(),
        P(),
    )
    out_specs = (pairs, spatial, pairs, spatial, heads, heads, heads) + (P(),) * 6
    return jax.shard_map(
        functools.partial(local, net),
        mesh=mesh,
        in_specs=in_specs,
        out_specs=out_specs,
        check_vma=False,
    )
```

```python
import functools
import math

import jax
import jax.numpy as jnp
import numpy as np
from jax import lax
from jax.experimental import pallas as pl
from jax.experimental.pallas import tpu as pltpu
from jax.sharding import PartitionSpec as P

C = 2048
MID = 512
ACTIONS = 18
ATOMS = 51
GROUPS = 32
SIDE = 11
PIX = SIDE * SIDE
BLOCKS = 2
MB = 2
STEP = 10
SEG = 64
HPAD = ACTIONS * SEG
HOUT = ACTIONS * ATOMS

bf16 = jnp.bfloat16
f32 = jnp.float32

eps_norm = 1e-05
decay_moment = 0.5
beta_second = 0.95
adam_eps = 1e-08
rate_muon = 0.2
decay_muon = 0.01
rate_head = 0.02
decay_head = 0.01
rate_gain = 0.05
clip_limit = 0.01
cql_alpha = 0.05
value_max = 3.0
coef_a = 3.4445
coef_b = -4.775
coef_c = 2.0315

FROWS = 128
FPB = 2
BROWS = FPB * FROWS
TAPS = [(dr, dc) for dr in (-1, 0, 1) for dc in (-1, 0, 1)]
MIB = 1024 * 1024


def tap_masks():
    pixel = np.arange(FROWS)
    row, col = pixel // SIDE, pixel % SIDE
    masks = [
        (pixel < PIX) & (row + dr >= 0) & (row + dr < SIDE) & (col + dc >= 0) & (col + dc < SIDE)
        for dr, dc in TAPS
    ]
    return np.repeat(np.stack(masks).astype(np.float32).reshape(9 * FROWS, 1), 128, axis=1)


class Net:
    def __init__(self, dp, ns):
        self.dp, self.ns = dp, ns
        self.ns_bits = [1 << i for i in range(ns.bit_length() - 1)]
        self.dp_bits = [1 << i for i in range(dp.bit_length() - 1)]
        self.plain = not (dp == 8 and ns == 4)

    def swap(self, value, axis, bit):
        pairs = []
        for d in range(self.dp):
            for n in range(self.ns):
                partner = (d ^ bit) * self.ns + n if axis == "dp" else d * self.ns + (n ^ bit)
                pairs.append((d * self.ns + n, partner))
        return lax.ppermute(value, ("dp", "ns"), pairs)

    def add_all(self, value, axes=("dp", "ns")):
        for axis in axes:
            for bit in self.dp_bits if axis == "dp" else self.ns_bits:
                value = value + self.swap(value, axis, bit)
        return value


def pick(value, index, axis):
    return lax.dynamic_index_in_dim(value, index, axis, keepdims=False)


def bit_of(index, shift):
    return lax.rem(lax.div(index, 1 << shift), 2)


def after(value, *deps):
    return lax.optimization_barrier((value,) + deps)[0]


class Run:
    def __init__(self, steps):
        self.steps, self.deps, self.done, self.value = steps, None, False, None

    def step(self, *deps):
        if self.done:
            return ()
        try:
            sent = self.steps.send(deps if self.deps else None)
            self.deps = True
            return tuple(sent)
        except StopIteration as end:
            self.done, self.value = True, end.value
            return ()


class Shards:
    def __init__(self, arrays, pieces):
        self.arrays, self.pieces = arrays, pieces


def own_half(own):
    core = bit_of(lax.axis_index("dp"), 0)
    return pick(own.reshape(2, own.shape[0] // 2, MID), core, 0)


def gather_direct(net, shard):
    own = shard.astype(bf16)
    if net.plain:
        return Run(at_once([Shards((lax.all_gather(own, "ns", axis=0, tiled=True),), None)]))
    return Run(gather_direct_steps(net, own))


def at_once(value):
    if value is None:
        yield ()
    return value


def gather_direct_steps(net, own):
    half = own_half(own)
    n = half.shape[0]
    got = tuple(net.swap(half, "ns", rel) for rel in (1, 2, 3))
    deps = yield (got[0],)
    got = tuple(after(v, *deps) for v in got)
    other = tuple(net.swap(v, "dp", 1) for v in got)
    deps = yield got
    pieces = [(0, 0, (0, None, 0, 2 * n), 2 * n)]
    for core in range(2):
        for rel in (1, 2, 3):
            pieces.append((core * 3 + rel, 0, (rel, core, 0, 2 * n), n))
    return [Shards((own,) + got + other, pieces)]


def gather_two(net, shards, *deps):
    owns = [v.astype(bf16) for v in shards]
    if net.plain:
        return Run(
            at_once([Shards((lax.all_gather(v, "ns", axis=0, tiled=True),), None) for v in owns])
        )
    return Run(gather_two_steps(net, owns, deps))


def gather_two_steps(net, owns, deps):
    halves = [own_half(v) for v in owns]
    sizes = [v.shape[0] // 2 for v in halves]
    rows = sum(sizes)
    sent = jnp.concatenate(
        [v[:n] for v, n in zip(halves, sizes, strict=True)]
        + [v[n:] for v, n in zip(halves, sizes, strict=True)],
        axis=0,
    )
    sent = after(sent, *deps) if deps else sent
    got_x, got_y = net.swap(sent, "ns", 1), net.swap(sent, "ns", 2)
    deps = yield (sent,)
    got_x, got_y = after(got_x, *deps), after(got_y, *deps)
    sent = got_x[:rows], got_y[rows:]
    got_a, got_b = net.swap(sent[0], "ns", 2), net.swap(sent[1], "ns", 1)
    other = net.swap(got_x, "dp", 1), net.swap(got_y, "dp", 1)
    deps = yield sent
    got_a, got_b = after(got_a, *deps), after(got_b, *deps)
    got = (got_x, got_y, got_a, got_b)
    other = other + (net.swap(got_a, "dp", 1), net.swap(got_b, "dp", 1))
    yield got
    out, start = [], 0
    for own, n in zip(owns, sizes, strict=True):
        pieces = [(0, 0, (0, None, 0, 4 * n), 4 * n)]
        for core in range(2):
            at = 1 + 4 * core
            for rel, k in ((1, at), (2, at + 1)):
                pieces.append((k, start, (rel, core, 0, 4 * n), n))
                pieces.append((k, rows + start, (rel, core, n, 4 * n), n))
            pieces.append((at + 2, start, (3, core, 0, 4 * n), n))
            pieces.append((at + 3, start, (3, core, n, 4 * n), n))
        out.append(Shards((own,) + got + other, pieces))
        start += n
    return out


def export_rows(shard, buffer, full, sems):
    if full is None:
        return lambda: None
    copy = pltpu.make_async_copy(buffer, full, sems.at[13])
    pl.when(pl.program_id(0) == 0)(copy.start)
    return lambda: pl.when(pl.program_id(0) == pl.num_programs(0) - 1)(copy.wait)


def row_copies(shard, refs, pos_ref, buffer, sems):
    if shard.pieces is None:
        return [pltpu.make_async_copy(refs[0], buffer, sems.at[0])]
    here, my_core = pos_ref[0], pos_ref[1]
    copies = []
    for q, (k, row, (rel, core, offset, each), n) in enumerate(shard.pieces):
        if core is None:
            place = here * each
        else:
            place = (here ^ rel) * each + (my_core ^ core) * (each // 2) + offset
        copies.append(
            pltpu.make_async_copy(
                refs[k].at[pl.ds(row, n)],
                buffer.at[pl.ds(pl.multiple_of(place, 16), n)],
                sems.at[q],
            )
        )
    return copies


def load_rows(shard, refs, pos_ref, buffer, sems):
    copies = row_copies(shard, refs, pos_ref, buffer, sems)
    for copy in copies:
        copy.start()
    for copy in copies:
        copy.wait()


def place_rows(shard, refs, pos_ref, full, buffer, sems):
    copies = row_copies(shard, refs, pos_ref, buffer, sems)
    out = pltpu.make_async_copy(buffer, full, sems.at[13])
    step = pl.program_id(0)

    @pl.when(step == 0)
    def _():
        for copy in copies:
            copy.start()

    @pl.when(step == 1)
    def _():
        for copy in copies:
            copy.wait()
        out.start()

    @pl.when(step == pl.num_programs(0) - 1)
    def _():
        out.wait()


class Share:
    def __init__(self, arrays, pieces):
        self.arrays, self.pieces = arrays, pieces

    def copies(self, refs, pos, buffer, start, sems, first):
        out = []
        for q, (k, row, core, path, n) in enumerate(self.pieces):
            if core is None:
                place = start + path * n
            else:
                place = start + ((pos[1] ^ core) * 2 + (pos[5] ^ path)) * n
                place = pl.multiple_of(place, 16)
            out.append(
                pltpu.make_async_copy(
                    refs[k].at[pl.ds(row, n)], buffer.at[pl.ds(place, n)], sems.at[first + q]
                )
            )
        return out


def vmem_call(kernel, name, ins, outs):
    return pl.pallas_call(
        kernel,
        name=name,
        in_specs=[pl.BlockSpec(memory_space=pltpu.SMEM)]
        + [pl.BlockSpec(memory_space=pltpu.VMEM)] * (len(ins) - 1),
        out_shape=[jax.ShapeDtypeStruct(shape, bf16) for shape in outs],
        cost_estimate=pl.CostEstimate(flops=1024, bytes_accessed=1024, transcendentals=0),
        compiler_params=pltpu.CompilerParams(vmem_limit_bytes=24 * MIB),
    )(*ins)


def split_kernel(count, pos, *refs):
    grads, (got, send_a, send_b, keep_a, keep_b) = refs[:count], refs[count:]
    core, x, y = pos[1], pos[3], pos[4]
    start = 0
    for g in grads:
        rows = pl.ds(start, g.shape[4])
        start += g.shape[4]
        for j in range(2):
            send_a[j, rows] = g[j, 1 - x, core, 0] + got[j, 1 - x, 0, rows]
            keep_a[j, rows] = g[j, x, core, 0] + got[j, x, 0, rows]
            send_b[j, rows] = g[1 - y, j, core, 1] + got[1 - y, j, 1, rows]
            keep_b[j, rows] = g[y, j, core, 1] + got[y, j, 1, rows]


def turn_kernel(pos, keep_a, keep_b, got_a, got_b, send_a, send_b, rest_a, rest_b):
    x, y = pos[3], pos[4]
    send_a[...] = keep_a[1 - y] + got_a[1 - y]
    send_b[...] = keep_b[1 - x] + got_b[1 - x]
    rest_a[...] = keep_a[y] + got_a[y]
    rest_b[...] = keep_b[x] + got_b[x]


def half_kernel(pos, rest_a, rest_b, got_a, got_b, send, keep):
    @pl.when(pos[5] == 0)
    def _():
        send[...] = rest_b[...] + got_b[...]
        keep[...] = rest_a[...] + got_a[...]

    @pl.when(pos[5] == 1)
    def _():
        send[...] = rest_a[...] + got_a[...]
        keep[...] = rest_b[...] + got_b[...]


def reduce_steps(net, pos, grads):
    if net.plain:
        out = []
        for g in grads:
            share = lax.psum_scatter(g.astype(f32), "ns", scatter_dimension=0, tiled=True)
            out.append(Share((lax.psum(share, "dp").astype(bf16),), [(0, 0, None, 0, share.shape[0])]))
        return out
    core = pos[1]

    def half(some, which):
        parts = [pick(g, which, 2) for g in some]
        return jnp.concatenate(parts, axis=3) if len(parts) > 1 else parts[0]

    grads = [g.reshape(2, 2, 2, 2, g.shape[0] // 16, MID) for g in grads]
    sent = half(grads, 1 - core)
    got = net.swap(sent, "dp", 1)
    deps = yield (sent,)
    got = after(got, *deps)
    sizes = [g.shape[4] for g in grads]
    n = sum(sizes)
    two, one = (2, n, MID), (n, MID)
    send_a, send_b, keep_a, keep_b = vmem_call(
        functools.partial(split_kernel, len(grads)), "split_sum", [pos, *grads, got], [two] * 4
    )
    got_a, got_b = net.swap(send_a, "ns", 1), net.swap(send_b, "ns", 2)
    deps = yield send_a, send_b
    got_a, got_b = after(got_a, *deps), after(got_b, *deps)
    send_a, send_b, rest_a, rest_b = vmem_call(
        turn_kernel, "turn_sum", [pos, keep_a, keep_b, got_a, got_b], [one] * 4
    )
    got_a, got_b = net.swap(send_a, "ns", 2), net.swap(send_b, "ns", 1)
    deps = yield send_a, send_b
    got_a, got_b = after(got_a, *deps), after(got_b, *deps)
    sent, kept = vmem_call(half_kernel, "half_sum", [pos, rest_a, rest_b, got_a, got_b], [one] * 2)
    got = net.swap(sent, "dp", 2)
    deps = yield (sent,)
    kept = kept + after(got, *deps)
    got = net.swap(kept, "dp", 4)
    deps = yield (kept,)
    kept = kept + after(got, *deps)
    given, kept_other = net.swap(kept, "dp", 2), net.swap(kept, "dp", 1)
    deps = yield (kept,)
    given = after(given, *deps)
    given_other = net.swap(given, "dp", 1)
    deps = yield (given,)
    kept_other, given_other = after(kept_other, *deps), after(given_other, *deps)
    out, start = [], 0
    for size in sizes:
        out.append(
            Share(
                (kept, given, kept_other, given_other),
                [(k, start, k // 2, k % 2, size) for k in range(4)],
            )
        )
        start += size
    return out


HALF = MID // 2
PACK = HALF + 32
PATH = PACK // 2


def gram_steps(net, packs):
    first, second = packs
    if net.plain:
        first, second = (lax.psum(v.astype(f32), "ns").astype(bf16) for v in packs)
        return first, second, net.swap(first, "dp", 1), net.swap(second, "dp", 1)
    got_a, got_b = net.swap(first, "ns", 1), net.swap(second, "ns", 2)
    deps = yield first, second
    first, second = first + after(got_a, *deps), second + after(got_b, *deps)
    got_a, got_b = net.swap(first, "ns", 2), net.swap(second, "ns", 1)
    deps = yield first, second
    first, second = first + after(got_a, *deps), second + after(got_b, *deps)
    other = net.swap(first, "dp", 1), net.swap(second, "dp", 1)
    deps = yield first, second
    return first, second, after(other[0], *deps), after(other[1], *deps)


def add_steps(net, value):
    for axis, bits in (("dp", net.dp_bits), ("ns", net.ns_bits)):
        for bit in bits:
            got = net.swap(value, axis, bit)
            deps = yield (value,)
            value = value + after(got, *deps)
    return value


def sigmoid(v):
    return 0.5 * jnp.tanh(0.5 * v) + 0.5


def group_sum(t, size):
    tiles = t.shape[1] // 128
    u = jnp.concatenate([t[:, j * 128 : (j + 1) * 128] for j in range(tiles)], axis=0)
    lane = lax.broadcasted_iota(jnp.int32, u.shape, 1)
    step = 1
    while step < size:
        u = u + jnp.where(
            (lane & step) == 0, pltpu.roll(u, 128 - step, 1), pltpu.roll(u, step, 1)
        )
        step *= 2
    return jnp.concatenate([u[8 * j : 8 * j + 8] for j in range(tiles)], axis=1)


class Norm:
    def __init__(self, ref, layer, part):
        self.ref, self.row, self.base = ref, 2 * layer, (0, MID, 2 * MID)[part]

    def row_of(self, row, lanes):
        return self.ref[row : row + 1, self.base + lanes.start : self.base + lanes.stop]

    def gain(self, lanes):
        return self.row_of(self.row, lanes)

    def bias(self, lanes):
        return self.row_of(self.row + 1, lanes)


def live_rows():
    return lax.broadcasted_iota(jnp.int32, (FROWS, 128), 0) < PIX


def norm_stats(st, size):
    sums = group_sum(st[...], size) * (1.0 / (PIX * size))
    mean = sums[0:FPB]
    spread = jnp.maximum(sums[FPB : 2 * FPB] - mean * mean, 0.0)
    return mean, lax.rsqrt(spread + eps_norm)


def add_stats(st, f, lanes, v):
    st[f : f + 1, lanes] = jnp.sum(v, axis=0, keepdims=True)
    st[FPB + f : FPB + f + 1, lanes] = jnp.sum(v * v, axis=0, keepdims=True)


def units(width):
    for j in range(width // 128):
        for f in range(FPB):
            yield f, pl.ds(f * FROWS, FROWS), slice(j * 128, (j + 1) * 128)


def first_step(body):
    pl.when(pl.program_id(0) == 0)(body)


def reduce_kernel(shard, also, layer, pos, x, gains, *rest):
    gb = Norm(gains, layer, 0)
    n = len(shard.arrays)
    refs, rest = rest[:n], rest[n:]
    if also is not None:
        n = len(also.arrays)
        place_rows(also, rest[:n], pos, rest[n + 4], *rest[-2:])
        rest = rest[n : n + 4] + rest[n + 5 : -2]
    h, xh, rs, full, buf, sems, acc, st = rest

    @first_step
    def _():
        load_rows(shard, refs, pos, buf, sems)
        st[...] = jnp.zeros_like(st)

    finish = export_rows(shard, buf, full, sems)
    for j in range(MID // 256):
        lanes = slice(j * 256, (j + 1) * 256)
        a = jnp.dot(x[...], buf[:, lanes], preferred_element_type=f32)
        acc[:, lanes] = a
        for f in range(FPB):
            add_stats(st, f, lanes, a[f * FROWS : (f + 1) * FROWS])
    norm_out(acc, st, gb, h, xh, rs)
    finish()


def norm_out(acc, st, gb, h, xh, rs):
    mean, rstd = norm_stats(st, MID // GROUPS)
    rs[...] = jnp.zeros_like(rs)
    rs[0:FPB] = rstd
    live = live_rows()
    for f, rows, lanes in units(MID):
        v = jnp.where(live, (acc[rows, lanes] - mean[f : f + 1, lanes]) * rstd[f : f + 1, lanes], 0.0)
        xh[rows, lanes] = v.astype(bf16)
        v = v * gb.gain(lanes) + gb.bias(lanes)
        h[rows, lanes] = jnp.where(live, v * sigmoid(v), 0.0).astype(bf16)


def spread_taps(src, masks, taps):
    for f, rows, lanes in units(MID):
        v = src[rows, lanes].astype(f32)
        for k, (dr, dc) in enumerate(TAPS):
            shift = -(dr * SIDE + dc)
            t = v if shift == 0 else pltpu.roll(v, shift % FROWS, 0)
            t = t * masks[k * FROWS : (k + 1) * FROWS]
            taps[rows, k * MID + lanes.start : k * MID + lanes.stop] = t.astype(bf16)


def conv_kernel(shard, also, layer, pos, src, masks, gains, *rest):
    gb = Norm(gains, layer, 1)
    n = len(shard.arrays)
    refs, rest = rest[:n], rest[n:]
    if also is not None:
        n = len(also.arrays)
        place_rows(also, rest[:n], pos, rest[n + 5], *rest[-2:])
        rest = rest[n : n + 5] + rest[n + 6 : -2]
    taps, u2, xh, rs, full, buf, sems, acc, st = rest

    @first_step
    def _():
        load_rows(shard, refs, pos, buf, sems)
        st[...] = jnp.zeros_like(st)

    finish = export_rows(shard, buf, full, sems)
    spread_taps(src, masks, taps)
    for j in range(MID // 256):
        lanes = slice(j * 256, (j + 1) * 256)
        a = jnp.dot(taps[...], buf[:, lanes], preferred_element_type=f32)
        acc[:, lanes] = a
        for f in range(FPB):
            add_stats(st, f, lanes, a[f * FROWS : (f + 1) * FROWS])
    norm_out(acc, st, gb, u2, xh, rs)
    finish()


def expand_kernel(shard, layer, last, pos, u2, x, gains, *rest):
    gb = Norm(gains, layer, 2)
    n = len(shard.arrays)
    refs, (xh, rs, out, full, buf, sems, acc, st) = rest[:n], rest[n:]

    @first_step
    def _():
        load_rows(shard, refs, pos, buf, sems)
        st[...] = jnp.zeros_like(st)

    finish = export_rows(shard, buf, full, sems)
    for j in range(C // 256):
        lanes = slice(j * 256, (j + 1) * 256)
        a = lax.dot_general(
            u2[...], buf[lanes, :], (((1,), (1,)), ((), ())), preferred_element_type=f32
        )
        acc[:, lanes] = a
        for f in range(FPB):
            add_stats(st, f, lanes, a[f * FROWS : (f + 1) * FROWS])
    mean, rstd = norm_stats(st, C // GROUPS)
    rs[...] = jnp.zeros_like(rs)
    rs[0:FPB] = rstd
    if last:
        out[...] = jnp.zeros_like(out)
    live = live_rows()
    for f, rows, lanes in units(C):
        v = jnp.where(live, (acc[rows, lanes] - mean[f : f + 1, lanes]) * rstd[f : f + 1, lanes], 0.0)
        xh[rows, lanes] = v.astype(bf16)
        v = x[rows, lanes].astype(f32) + (v * gb.gain(lanes) + gb.bias(lanes))
        v = jnp.where(live, v * sigmoid(v), 0.0)
        if last:
            out[f : f + 1, lanes] = jnp.sum(v, axis=0, keepdims=True) * (1.0 / PIX)
        else:
            out[rows, lanes] = v.astype(bf16)
    finish()


def back_sums(st, f, lanes, dv, xhat, gain, gacc):
    by_gain = jnp.sum(dv * xhat, axis=0, keepdims=True)
    by_bias = jnp.sum(dv, axis=0, keepdims=True)
    st[f : f + 1, lanes] = by_bias * gain
    st[FPB + f : FPB + f + 1, lanes] = by_gain * gain
    gacc[0:1, lanes] += by_gain
    gacc[1:2, lanes] += by_bias


def back_norm(st, size):
    sums = group_sum(st[...], size) * (1.0 / (PIX * size))
    return sums[0:FPB], sums[FPB : 2 * FPB]


def act_back(acc, st, xh, rs, gb, gacc, out):
    live = live_rows()
    for f, rows, lanes in units(MID):
        xhat = xh[rows, lanes].astype(f32)
        v = xhat * gb.gain(lanes) + gb.bias(lanes)
        s = sigmoid(v)
        dv = jnp.where(live, acc[rows, lanes] * (s + v * s * (1.0 - s)), 0.0)
        acc[rows, lanes] = dv
        back_sums(st, f, lanes, dv, xhat, gb.gain(lanes), gacc)
    m1, m2 = back_norm(st, MID // GROUPS)
    for f, rows, lanes in units(MID):
        xhat = xh[rows, lanes].astype(f32)
        da = rs[f : f + 1, lanes] * (
            acc[rows, lanes] * gb.gain(lanes) - m1[f : f + 1, lanes] - xhat * m2[f : f + 1, lanes]
        )
        out[rows, lanes] = jnp.where(live, da, 0.0).astype(bf16)


def tail_back_kernel(shard, layer, last, pos, d, x, xh3, rs3, xh2, rs2, gains, *rest):
    gb3, gb2 = Norm(gains, layer, 2), Norm(gains, layer, 1)
    n = len(shard.arrays)
    refs, (r, da3, da2, gacc3, gacc2, buf, sems, acc, st, acc2, st2) = rest[:n], rest[n:]

    @first_step
    def _():
        load_rows(shard, refs, pos, buf, sems)
        st[...] = jnp.zeros_like(st)
        st2[...] = jnp.zeros_like(st2)
        gacc3[...] = jnp.zeros_like(gacc3)
        gacc2[...] = jnp.zeros_like(gacc2)

    live = live_rows()
    for f, rows, lanes in units(C):
        xhat = xh3[rows, lanes].astype(f32)
        v = x[rows, lanes].astype(f32) + (xhat * gb3.gain(lanes) + gb3.bias(lanes))
        s = sigmoid(v)
        grad = d[f : f + 1, lanes] if last else d[rows, lanes].astype(f32)
        dv = jnp.where(live, grad * (s + v * s * (1.0 - s)), 0.0)
        acc[rows, lanes] = dv
        r[rows, lanes] = dv.astype(bf16)
        back_sums(st, f, lanes, dv, xhat, gb3.gain(lanes), gacc3)
    m1, m2 = back_norm(st, C // GROUPS)
    for f, rows, lanes in units(C):
        xhat = xh3[rows, lanes].astype(f32)
        da = rs3[f : f + 1, lanes] * (
            acc[rows, lanes] * gb3.gain(lanes) - m1[f : f + 1, lanes] - xhat * m2[f : f + 1, lanes]
        )
        da3[rows, lanes] = jnp.where(live, da, 0.0).astype(bf16)
    for j in range(MID // 256):
        lanes = slice(j * 256, (j + 1) * 256)
        acc2[:, lanes] = jnp.dot(da3[...], buf[:, lanes], preferred_element_type=f32)
    act_back(acc2, st2, xh2, rs2, gb2, gacc2, da2)


def conv_back_kernel(shard, shard_one, layer, pos, da2, masks, xh1, rs1, gains, *rest):
    gb1 = Norm(gains, layer, 0)
    n = len(shard.arrays)
    refs, rest = rest[:n], rest[n:]
    if shard_one is not None:
        n = len(shard_one.arrays)
        refs_one, (r, da1, gacc1, d, buf, sems, taps, acc, st, buf_one, sems_one) = rest[:n], rest[n:]
    else:
        da1, gacc1, buf, sems, taps, acc, st = rest

    @first_step
    def _():
        load_rows(shard, refs, pos, buf, sems)
        if shard_one is not None:
            load_rows(shard_one, refs_one, pos, buf_one, sems_one)
        st[...] = jnp.zeros_like(st)
        gacc1[...] = jnp.zeros_like(gacc1)

    spread_taps(da2, masks, taps)
    for j in range(MID // 256):
        total = None
        for k in range(9):
            part = lax.dot_general(
                taps[:, (8 - k) * MID : (9 - k) * MID],
                buf[k * MID + j * 256 : k * MID + (j + 1) * 256, :],
                (((1,), (1,)), ((), ())),
                preferred_element_type=f32,
            )
            total = part if total is None else total + part
        acc[:, j * 256 : (j + 1) * 256] = total
    act_back(acc, st, xh1, rs1, gb1, gacc1, da1)
    if shard_one is not None:
        for j in range(C // 256):
            lanes = slice(j * 256, (j + 1) * 256)
            a = lax.dot_general(
                da1[...], buf_one[lanes, :], (((1,), (1,)), ((), ())), preferred_element_type=f32
            )
            d[:, lanes] = (r[:, lanes].astype(f32) + a).astype(bf16)


def rows_spec(width):
    return pl.BlockSpec((BROWS, width), lambda i: (i, 0))


def eight_spec(width):
    return pl.BlockSpec((8, width), lambda i: (i, 0))


def gains_spec():
    return whole_spec(2 * BLOCKS, 2 * MID + C)


def whole_spec(rows, width):
    return pl.BlockSpec((rows, width), lambda i: (0, 0))


HBM = pl.BlockSpec(memory_space=pltpu.HBM)
ANY = pl.BlockSpec(memory_space=pl.ANY)
SMEM = pl.BlockSpec(memory_space=pltpu.SMEM)


def kept_sds(rows, width, dtype):
    return pltpu.HBM((rows, width), dtype)


def sds(rows, width, dtype):
    return jax.ShapeDtypeStruct((rows, width), dtype)


def call(kernel, name, rows, in_specs, outs, scratch, limit=48):
    return pl.pallas_call(
        kernel,
        name=name,
        grid=(rows // BROWS,),
        in_specs=in_specs,
        out_specs=[spec for _, spec in outs],
        out_shape=[shape for shape, _ in outs],
        scratch_shapes=scratch,
        cost_estimate=pl.CostEstimate(flops=1024, bytes_accessed=1024, transcendentals=0),
        compiler_params=pltpu.CompilerParams(
            vmem_limit_bytes=limit * MIB, dimension_semantics=("arbitrary",)
        ),
    )


def row_sems():
    return pltpu.SemaphoreType.DMA((14,))


def run_reduce(pos, x, shard, gains, layer, also=None):
    rows = x.shape[0]
    more = also.arrays if also else ()
    eights = rows // BROWS * 8
    return call(
        functools.partial(reduce_kernel, shard, also, layer),
        "reduce_norm",
        rows,
        [SMEM, rows_spec(C), gains_spec()] + [ANY] * (len(shard.arrays) + len(more)),
        [
            (sds(rows, MID, bf16), rows_spec(MID)),
            (kept_sds(rows, MID, bf16), rows_spec(MID)),
            (kept_sds(eights, MID, f32), eight_spec(MID)),
            (kept_sds(C, MID, bf16), HBM),
        ]
        + ([(kept_sds(9 * MID, MID, bf16), HBM)] if also else []),
        [
            pltpu.VMEM((C, MID), bf16),
            row_sems(),
            pltpu.VMEM((BROWS, MID), f32),
            pltpu.VMEM((8, MID), f32),
        ]
        + ([pltpu.VMEM((9 * MID, MID), bf16), row_sems()] if also else []),
    )(pos, x, gains, *shard.arrays, *more)


def run_conv(pos, h, masks, shard, gains, layer, also=None):
    rows = h.shape[0]
    more = also.arrays if also else ()
    eights = rows // BROWS * 8
    return call(
        functools.partial(conv_kernel, shard, also, layer),
        "conv_norm",
        rows,
        [SMEM, rows_spec(MID), whole_spec(9 * FROWS, 128), gains_spec()]
        + [ANY] * (len(shard.arrays) + len(more)),
        [
            (kept_sds(rows, 9 * MID, bf16), rows_spec(9 * MID)),
            (sds(rows, MID, bf16), rows_spec(MID)),
            (kept_sds(rows, MID, bf16), rows_spec(MID)),
            (kept_sds(eights, MID, f32), eight_spec(MID)),
            (kept_sds(9 * MID, MID, bf16), HBM),
        ]
        + ([(kept_sds(C, MID, bf16), HBM)] if also else []),
        [
            pltpu.VMEM((9 * MID, MID), bf16),
            row_sems(),
            pltpu.VMEM((BROWS, MID), f32),
            pltpu.VMEM((8, MID), f32),
        ]
        + ([pltpu.VMEM((C, MID), bf16), row_sems()] if also else []),
    )(pos, h, masks, gains, *shard.arrays, *more)


def run_expand(pos, u2, x, shard, gains, layer, last):
    rows = x.shape[0]
    eights = rows // BROWS * 8
    return call(
        functools.partial(expand_kernel, shard, layer, last),
        "expand_norm",
        rows,
        [SMEM, rows_spec(MID), rows_spec(C), gains_spec()] + [ANY] * len(shard.arrays),
        [
            (kept_sds(rows, C, bf16), rows_spec(C)),
            (kept_sds(eights, C, f32), eight_spec(C)),
            (sds(eights, C, f32), eight_spec(C)) if last else (sds(rows, C, bf16), rows_spec(C)),
            (kept_sds(C, MID, bf16), HBM),
        ],
        [
            pltpu.VMEM((C, MID), bf16),
            row_sems(),
            pltpu.VMEM((BROWS, C), f32),
            pltpu.VMEM((8, C), f32),
        ],
    )(pos, u2, x, gains, *shard.arrays)


def run_tail_back(pos, d, x, xh3, rs3, xh2, rs2, gains, shard, layer, last):
    rows = x.shape[0]
    return call(
        functools.partial(tail_back_kernel, shard, layer, last),
        "tail_back",
        rows,
        [
            SMEM,
            eight_spec(C) if last else rows_spec(C),
            rows_spec(C),
            rows_spec(C),
            eight_spec(C),
            rows_spec(MID),
            eight_spec(MID),
            gains_spec(),
        ]
        + [HBM] * len(shard.arrays),
        [
            (sds(rows, C, bf16), rows_spec(C)),
            (sds(rows, C, bf16), rows_spec(C)),
            (sds(rows, MID, bf16), rows_spec(MID)),
            (sds(8, C, f32), whole_spec(8, C)),
            (sds(8, MID, f32), whole_spec(8, MID)),
        ],
        [
            pltpu.VMEM((C, MID), bf16),
            row_sems(),
            pltpu.VMEM((BROWS, C), f32),
            pltpu.VMEM((8, C), f32),
            pltpu.VMEM((BROWS, MID), f32),
            pltpu.VMEM((8, MID), f32),
        ],
    )(pos, d, x, xh3, rs3, xh2, rs2, gains, *shard.arrays)


def run_conv_back(pos, da2, masks, xh1, rs1, gains, shard, shard_one, r, layer):
    rows = da2.shape[0]
    more = shard_one is not None
    extra = shard_one.arrays if more else ()
    return call(
        functools.partial(conv_back_kernel, shard, shard_one, layer),
        "conv_back",
        rows,
        [
            SMEM,
            rows_spec(MID),
            whole_spec(9 * FROWS, 128),
            rows_spec(MID),
            eight_spec(MID),
            gains_spec(),
        ]
        + [HBM] * (len(shard.arrays) + len(extra))
        + ([rows_spec(C)] if more else []),
        [
            (sds(rows, MID, bf16), rows_spec(MID)),
            (sds(8, MID, f32), whole_spec(8, MID)),
        ]
        + ([(sds(rows, C, bf16), rows_spec(C))] if more else []),
        [
            pltpu.VMEM((9 * MID, MID), bf16),
            row_sems(),
            pltpu.VMEM((BROWS, 9 * MID), bf16),
            pltpu.VMEM((BROWS, MID), f32),
            pltpu.VMEM((8, MID), f32),
        ]
        + ([pltpu.VMEM((C, MID), bf16), row_sems()] if more else []),
        28,
    )(pos, da2, masks, xh1, rs1, gains, *shard.arrays, *extra, *([r] if more else []))


def head_in_kernel(width, pos, feats, head, rows_out, logits, meta_out, select_out):
    everyone, slots = feats.shape[0], rows_out.shape[0]
    meta = feats[:, width : width + 128]
    match = meta[:, 2:3].astype(f32) == pos[2].astype(f32)
    ones = jnp.where(match, 1.0, 0.0)
    row = lax.broadcasted_iota(jnp.int32, (everyone, everyone), 0)
    col = lax.broadcasted_iota(jnp.int32, (everyone, everyone), 1)
    earlier = jnp.where(col < row, 1.0, 0.0).astype(bf16)
    place = jnp.dot(
        earlier,
        jnp.broadcast_to(ones, (everyone, 128)).astype(bf16),
        preferred_element_type=f32,
    )[:, 0:1]
    slot = lax.broadcasted_iota(jnp.int32, (everyone, slots), 1).astype(f32)
    select = jnp.where((slot == place) & match, 1.0, 0.0).astype(bf16)
    select_out[...] = select
    turn = (((0,), (0,)), ((), ()))
    rows = lax.dot_general(select, feats[:, :width], turn, preferred_element_type=f32).astype(bf16)
    rows_out[...] = rows
    meta_out[...] = lax.dot_general(select, meta, turn, preferred_element_type=f32)
    logits[...] = jnp.dot(rows, head[...], preferred_element_type=f32)


def head_loss_kernel(logits, meta, head, select, grad_out, back, loss, probs):
    count = logits.shape[0]
    lane = lax.broadcasted_iota(jnp.int32, (count, 128), 1)
    spot = lane & (SEG - 1)
    level = value_max * (spot.astype(f32) * (2.0 / (ATOMS - 1)) - 1.0)
    values = jnp.zeros((count, 128), f32)
    columns = []
    for a in range(ACTIONS):
        chunk = slice(a // 2 * 128, a // 2 * 128 + 128)
        inside = (lane >= (a % 2) * SEG) & (lane < (a % 2) * SEG + ATOMS)
        v = logits[:, chunk]
        top = jnp.max(jnp.where(inside, v, -3.0e38), axis=1, keepdims=True)
        e = jnp.where(inside, jnp.exp(jnp.minimum(v - top, 0.0)), 0.0)
        p = e / jnp.sum(e, axis=1, keepdims=True)
        q = jnp.sum(p * level, axis=1, keepdims=True)
        columns.append(q)
        values = jnp.where(lane == a, q, values)
        if a % 2 == 0:
            probs[:, chunk] = p
        else:
            probs[:, chunk] += p
    target, weight, action = meta[:, 0:1], meta[:, 1:2], meta[:, 3:4]
    real = lane < ACTIONS
    hot = (lane.astype(f32) == action).astype(f32)
    chosen = jnp.sum(values * hot, axis=1, keepdims=True)
    top = jnp.max(jnp.where(real, values, -3.0e38), axis=1, keepdims=True)
    e = jnp.where(real, jnp.exp(jnp.minimum(values - top, 0.0)), 0.0)
    total = jnp.sum(e, axis=1, keepdims=True)
    soft_top = top + jnp.log(total)
    row_loss = weight * ((chosen - target) * (chosen - target) + cql_alpha * (soft_top - chosen))
    loss[...] = jnp.zeros(loss.shape, f32) + jnp.sum(row_loss, axis=0, keepdims=True)
    slope = weight * (2.0 * (chosen - target) * hot + cql_alpha * (e / total - hot))
    for j in range(ACTIONS // 2):
        chunk = slice(j * 128, j * 128 + 128)
        low = lane < SEG
        q = jnp.where(low, columns[2 * j], columns[2 * j + 1])
        s = jnp.where(low, slope[:, 2 * j : 2 * j + 1], slope[:, 2 * j + 1 : 2 * j + 2])
        grad_out[:, chunk] = (s * probs[:, chunk] * (level - q)).astype(bf16)
    feat = lax.dot_general(
        grad_out[...], head[...], (((1,), (1,)), ((), ())), preferred_element_type=f32
    ).astype(bf16)
    back[...] = jnp.dot(select[...], feat, preferred_element_type=f32).astype(bf16)


def plain_call(kernel, name, outs, scratch, limit=48):
    return pl.pallas_call(
        kernel,
        name=name,
        out_shape=outs,
        scratch_shapes=scratch,
        compiler_params=pltpu.CompilerParams(vmem_limit_bytes=limit * MIB),
    )


def adam_step(weight, first, second, grad_in, rate, decay):
    first_new = decay_moment * first + (1.0 - decay_moment) * grad_in
    second_new = beta_second * second + (1.0 - beta_second) * grad_in * grad_in
    normed = (
        first_new
        / (1.0 - decay_moment**STEP)
        / (jnp.sqrt(second_new / (1.0 - beta_second**STEP)) + adam_eps)
    )
    return (weight - rate * (normed + decay * weight), first_new, second_new)


def heads_kernel(factor, weight, first, second, grad, *outs):
    values = adam_step(
        weight[...], first[...], second[...], factor[0] * grad[...], rate_head, decay_head
    )
    for out, value in zip(outs, values, strict=True):
        out[...] = value


def heads_step(factor, arrays):
    width = arrays[0].shape[2]
    spec = pl.BlockSpec((HOUT // 6, 1, width), lambda i: (i, 0, 0))
    return pl.pallas_call(
        heads_kernel,
        name="heads",
        grid=(6,),
        in_specs=[SMEM] + [spec] * 4,
        out_specs=[spec] * 3,
        out_shape=[jax.ShapeDtypeStruct((HOUT, 1, width), f32)] * 3,
        compiler_params=pltpu.CompilerParams(vmem_limit_bytes=63 * MIB),
    )(factor.reshape(1), *arrays)


def gram(a, b):
    return jnp.einsum("ri,rj->ij", a, b, preferred_element_type=f32)


def weight_grad(a, b):
    return jnp.einsum("ri,rj->ij", a, b, preferred_element_type=f32).astype(bf16)


TURN = (((0,), (0,)), ((), ()))


def turned_dot(a, b):
    return lax.dot_general(a, b, TURN, preferred_element_type=f32)


def pack_to(out_a, out_b, slot, core, upper, lower):
    row = lax.broadcasted_iota(jnp.int32, (HALF, MID), 0) + core * HALF
    col = lax.broadcasted_iota(jnp.int32, (HALF, MID), 1)
    body = jnp.where(row < col, upper, lower).astype(bf16)
    diag = jnp.sum(jnp.where(row == col, upper, 0.0), axis=0, keepdims=True)
    out_a[slot] = body[:PATH]
    out_b[slot, : HALF - PATH] = body[PATH:]
    out_b[slot, HALF - PATH :] = jnp.broadcast_to(diag, (PACK - HALF, MID)).astype(bf16)


def rows_of(ref, k):
    n = ref.shape[0] // 4 if k < 4 else ref.shape[0] // 2
    return ref.at[pl.ds((k if k < 4 else k - 4) * n, n)], n


def core_columns(core):
    return pl.ds(pl.multiple_of(core * HALF, HALF), HALF)


def old_gram_kernel(pos, pair, spatial, out_a, out_b, buf, low, sems):
    core = pos[1]
    mine = core_columns(core)
    copies, spans, at = [], [], 0
    for k in range(6):
        src, n = rows_of(pair if k < 4 else spatial, k)
        spans.append(slice(at, at + n))
        copies.append(pltpu.make_async_copy(src, buf.at[pl.ds(at, n)], sems.at[k]))
        at += n
    for copy in copies:
        copy.start()
    for k in range(6):
        copies[k].wait()
        low[spans[k]] = buf[spans[k]].astype(bf16)
    for p in range(3):
        upper, lower = (turned_dot(low[spans[k], mine], low[spans[k]]) for k in (2 * p, 2 * p + 1))
        pack_to(out_a, out_b, p, core, upper, lower)


def cross_gram_kernel(shares, pos, pair, spatial, *rest):
    refs, (out_a, out_b, full, buf, share, low, sems) = rest[:-7], rest[-7:]
    core = pos[1]
    mine = core_columns(core)
    copies, spans, at, used = [], [], 0, 0
    for s, (k, got) in enumerate(shares.items()):
        src, n = rows_of(pair if k < 4 else spatial, k)
        spans.append(slice(at, at + n))
        group = [pltpu.make_async_copy(src, buf.at[pl.ds(at, n)], sems.at[5 * s])]
        here = refs[used : used + len(got.arrays)]
        used += len(got.arrays)
        group += got.copies(here, pos, share, at, sems, 5 * s + 1)
        copies.append(group)
        at += n
    for group in copies:
        for copy in group:
            copy.start()
    for s, span in enumerate(spans):
        for copy in copies[s]:
            copy.wait()
        if s == len(spans) - 1:
            export = pltpu.make_async_copy(share, full, sems.at[5 * len(spans)])
            export.start()
        low[span] = buf[span].astype(bf16)
        upper = turned_dot(low[span, mine], share[span]) + turned_dot(share[span, mine], low[span])
        pack_to(out_a, out_b, s, core, upper, turned_dot(share[span, mine], share[span]))
    export.wait()


def gram_call(kernel, name, pos, moms, arrays, rows, count, scratch, sems, outs=()):
    return pl.pallas_call(
        kernel,
        name=name,
        in_specs=[SMEM, HBM, HBM] + [ANY] * len(arrays),
        out_specs=[pl.BlockSpec(memory_space=pltpu.VMEM)] * 2 + [HBM] * len(outs),
        out_shape=[jax.ShapeDtypeStruct((count, PATH, MID), bf16)] * 2 + list(outs),
        scratch_shapes=[pltpu.VMEM((rows, MID), f32)]
        + [pltpu.VMEM((rows, MID), bf16)] * scratch
        + [pltpu.SemaphoreType.DMA((sems,))],
        cost_estimate=pl.CostEstimate(flops=1024, bytes_accessed=1024, transcendentals=0),
        compiler_params=pltpu.CompilerParams(vmem_limit_bytes=28 * MIB),
    )(pos, *moms, *arrays)


def old_grams(pos, moms):
    rows = moms[0].shape[0] + moms[1].shape[0]
    return gram_call(old_gram_kernel, "old_gram", pos, moms, [], rows, 3, 1, 6)


def cross_grams(pos, moms, shares):
    rows = sum(moms[0].shape[0] // 4 if k < 4 else moms[1].shape[0] // 2 for k in shares)
    return gram_call(
        functools.partial(cross_gram_kernel, shares),
        "cross_gram",
        pos,
        moms,
        [v for share in shares.values() for v in share.arrays],
        rows,
        len(shares),
        2,
        5 * len(shares) + 1,
        [kept_sds(rows, MID, bf16)],
    )


def newton_kernel(groups, pos, facts, *rest):
    counts, order = tuple(len(g) for g in groups), [k for g in groups for k in g]
    n = 4 * (1 + len(counts))
    packs, rest = rest[:n], rest[n:]
    weights, moms, rest = rest[0:2], rest[2:4], rest[4:]
    shares, rest = rest[: len(groups)], rest[len(groups) :]
    news, moments, report, rest = rest[0:2], rest[2:4], rest[4], rest[5:]
    olds, crosses, w_buf, m_buf, g_buf, poly, sems, big_sems, share_sems, out_sems = rest
    pair_rows, rows = weights[0].shape[0], w_buf.shape[0]
    core = pos[1]
    spans, at = [], 0
    for k in range(6):
        count = pair_rows // 4 if k < 4 else (rows - pair_rows) // 2
        spans.append((at, count))
        at += count

    small = []
    at = 0
    for q, count in enumerate((3,) + counts):
        buffer = olds if q == 0 else crosses
        for j in range(4):
            side = core if j < 2 else 1 - core
            small.append(
                pltpu.make_async_copy(
                    packs[4 * q + j],
                    buffer.at[side, pl.ds(at, count), pl.ds(j % 2 * PATH, PATH)],
                    sems.at[4 * q + j],
                )
            )
        at = 0 if q == 0 else at + count
    big = []
    for q, (src, dst) in enumerate(((weights, w_buf), (moms, m_buf))):
        big.append(pltpu.make_async_copy(src[0], dst.at[pl.ds(0, pair_rows)], big_sems.at[2 * q]))
        big.append(
            pltpu.make_async_copy(
                src[1], dst.at[pl.ds(pair_rows, rows - pair_rows)], big_sems.at[2 * q + 1]
            )
        )
    for ids, share in zip(groups, shares, strict=True):
        at = 0
        for k in ids:
            start, n = spans[k]
            big.append(
                pltpu.make_async_copy(
                    share.at[pl.ds(at, n)], g_buf.at[pl.ds(start, n)], share_sems.at[k]
                )
            )
            at += n
    for copy in small:
        copy.start()
    for copy in small:
        copy.wait()
    for copy in big:
        copy.start()

    row = lax.broadcasted_iota(jnp.int32, (MID, MID), 0)
    col = lax.broadcasted_iota(jnp.int32, (MID, MID), 1)
    above, on = row < col, row == col

    def total(v):
        return jnp.sum(jnp.sum(v, axis=0, keepdims=True), axis=1, keepdims=True)

    def pack_of(buffer, p):
        body = jnp.concatenate([buffer[0, p, 0:HALF], buffer[1, p, 0:HALF]], axis=0).astype(f32)
        diag = (
            buffer[0, p, HALF : HALF + 16].astype(f32) + buffer[1, p, HALF : HALF + 16].astype(f32)
        )
        return body, diag[0:1]

    def diag_of(body):
        return jnp.sum(jnp.where(on, body, 0.0), axis=0, keepdims=True)

    squares = jnp.zeros((1, 1), f32)
    for p in range(6):
        squares = squares + total(jnp.where(on, pack_of(crosses, p)[0], 0.0))
    weight_total = jnp.zeros((1, 1), f32) + facts[1]
    grad_norm = jnp.sqrt(squares + facts[0]) / weight_total
    factor = jnp.minimum(1.0, clip_limit / grad_norm) / weight_total
    lane = lax.broadcasted_iota(jnp.int32, report.shape, 1)
    report[...] = jnp.where(lane == 0, grad_norm, factor)

    def low_dot(a, b):
        return jnp.dot(a.astype(bf16), b.astype(bf16), preferred_element_type=f32)

    scales = []
    for k in range(6):
        old, old_diag = pack_of(olds, k // 2)
        body, cross_diag = pack_of(crosses, order.index(k))
        quarter, half_factor = decay_moment * decay_moment, decay_moment * factor
        if k % 2 == 0:
            part = jnp.where(above, quarter * old + half_factor * body, (factor * factor) * body)
        else:
            old_diag = diag_of(old)
            part = jnp.where(above, half_factor * body, quarter * old + (factor * factor) * body)
        diag = quarter * old_diag + half_factor * cross_diag + (factor * factor) * diag_of(body)
        part = jnp.where(on, 0.5 * diag, part)
        g = part + part.T
        frob = jnp.sqrt(jnp.maximum(jnp.sum(diag, axis=1, keepdims=True), 0.0))
        scale = 1.0 / (frob + 1e-07)
        scales.append(scale)
        g0 = g * (scale * scale)
        e1 = coef_b * g0 + coef_c * low_dot(g0, g0)
        h = coef_a * g0 + low_dot(g0, e1)
        g1 = coef_a * h + low_dot(h, e1)
        e2 = coef_b * g1 + coef_c * low_dot(g1, g1)
        poly[k] = (coef_a * (e1 + e2) + low_dot(e1, e2)).astype(bf16)

    for copy in big:
        copy.wait()
    outs = []
    for k in range(6):
        start, count = spans[k]
        gain = 0.2 * math.sqrt(C if k < 4 else 9 * MID)
        chunk = 256 if count % 256 == 0 else 128 if count % 128 == 0 else 32
        for j in range(count // chunk):
            here = slice(start + j * chunk, start + (j + 1) * chunk)
            moment = decay_moment * m_buf[here] + factor * g_buf[here].astype(f32)
            m_buf[here] = moment
            current = moment * scales[k]
            ortho = (coef_a * coef_a) * current + jnp.dot(
                current.astype(bf16), poly[k], preferred_element_type=f32
            )
            w_buf[here] = (1.0 - rate_muon * decay_muon) * w_buf[here] - (rate_muon * gain) * ortho
        which, base = (0, 0) if k < 4 else (1, pair_rows)
        for q, (buf, dst) in enumerate(((w_buf, news), (m_buf, moments))):
            copy = pltpu.make_async_copy(
                buf.at[pl.ds(start, count)],
                dst[which].at[pl.ds(start - base, count)],
                out_sems.at[2 * k + q],
            )
            copy.start()
            outs.append(copy)
    for copy in outs:
        copy.wait()


def newton(pos, facts, olds, groups, crosses, weights, moms, shares):
    rows = weights[0].shape[0] + weights[1].shape[0]
    packs = [v for group in (olds, *crosses) for v in group]
    return pl.pallas_call(
        functools.partial(newton_kernel, groups),
        name="newton",
        in_specs=[SMEM, SMEM]
        + [HBM] * len(packs)
        + [HBM] * (4 + len(shares)),
        out_specs=[HBM] * 4 + [pl.BlockSpec(memory_space=pltpu.VMEM)],
        out_shape=[jax.ShapeDtypeStruct(w.shape, f32) for w in weights] * 2 + [sds(8, 128, f32)],
        scratch_shapes=[
            pltpu.VMEM((2, 3, PACK, MID), bf16),
            pltpu.VMEM((2, 6, PACK, MID), bf16),
            pltpu.VMEM((rows, MID), f32),
            pltpu.VMEM((rows, MID), f32),
            pltpu.VMEM((rows, MID), bf16),
            pltpu.VMEM((6, MID, MID), bf16),
            pltpu.SemaphoreType.DMA((len(packs),)),
            pltpu.SemaphoreType.DMA((4,)),
            pltpu.SemaphoreType.DMA((6,)),
            pltpu.SemaphoreType.DMA((12,)),
        ],
        compiler_params=pltpu.CompilerParams(vmem_limit_bytes=63 * MIB),
    )(pos, facts, *packs, *weights, *moms, *shares)


def local(
    net,
    frames,
    game_ids,
    actions,
    groups,
    targets,
    w_pair,
    w_spatial,
    mom_pair,
    mom_spatial,
    head_table,
    head_first,
    head_second,
    norm_params,
    norm_first,
    norm_second,
):
    dp_idx, ns_idx = lax.axis_index("dp"), lax.axis_index("ns")
    pos = jnp.stack(
        [ns_idx, bit_of(dp_idx, 0), dp_idx, bit_of(ns_idx, 0), bit_of(ns_idx, 1), bit_of(dp_idx, 1)]
    ).astype(jnp.int32)
    dev_rows = frames.shape[1]
    samples = MB * dev_rows
    rows = samples * FROWS
    devices = net.dp * net.ns
    everyone = devices * samples
    slots = MB * net.dp * (2 * net.ns * dev_rows // net.dp)
    col_width = C // net.ns

    get_a = gather_direct(net, w_pair[0, 0])
    get_a.step()

    masks = jnp.asarray(tap_masks())
    stream = jnp.pad(
        frames.reshape(samples, PIX, C), ((0, 0), (0, FROWS - PIX), (0, 0))
    ).reshape(rows, C)
    gains = norm_params.reshape(2 * BLOCKS, 2 * MID + C)
    x0 = stream
    got = get_a.step()
    get_b = gather_two(net, [w_spatial[0], w_pair[0, 1]], *got)
    sent = get_b.step()
    get_a.step()
    h, xh1, rs1, one = run_reduce(pos, after(x0, *sent), get_a.value[0], gains, 0)
    sent = get_b.step(h)

    out_col = jnp.arange(HOUT, dtype=jnp.int32)
    widen = (
        (out_col // ATOMS * SEG + out_col % ATOMS)[:, None] == jnp.arange(HPAD, dtype=jnp.int32)
    ).astype(bf16)
    head = jnp.dot(after(head_table, *sent)[0].astype(bf16), widen, preferred_element_type=f32).astype(bf16)

    moms = [mom_pair.reshape(-1, MID), mom_spatial.reshape(-1, MID)]
    old = old_grams(after(pos, *sent), moms)

    get_c = gather_two(net, [w_pair[1, 0], w_spatial[1]], *sent)
    sent = get_c.step()
    h = after(h, *old, head)
    get_b.step(*sent)
    get_b.step()
    kept = [(x0, xh1, rs1)]
    ones, mids, lasts = [one], [], []
    taps, u2, xh2, rs2, mid, last = run_conv(
        pos, h, masks, get_b.value[0], gains, 0, get_b.value[1]
    )
    sent = get_c.step(u2)
    get_d = gather_two(net, [w_pair[1, 1]], *sent)
    sent = get_d.step()
    xh3, rs3, x1, _ = run_expand(
        pos, after(u2, *sent), x0, Shards((last,), None), gains, 0, False
    )
    kept[0] = kept[0] + (taps, u2, xh2, rs2, xh3, rs3)
    mids.append(mid)
    lasts.append(last)
    get_c.step(x1)
    get_c.step()
    sent = get_d.step(x1)
    h, xh1, rs1, one, mid = run_reduce(
        pos, after(x1, *sent), get_c.value[0], gains, 1, get_c.value[1]
    )
    taps, u2, xh2, rs2, _ = run_conv(pos, h, masks, Shards((mid,), None), gains, 1)
    get_d.step(h)
    get_d.step()
    xh3, rs3, stream, last = run_expand(pos, u2, x1, get_d.value[0], gains, 1, True)
    kept.append((x1, xh1, rs1, taps, u2, xh2, rs2, xh3, rs3))
    ones, mids, lasts = [
        [Shards((v,), None) for v in pair]
        for pair in ((ones[0], one), (mids[0], mid), (lasts[0], last))
    ]
    pooled = stream.reshape(-1, 8, C)[:, :FPB].reshape(samples, C).astype(bf16)

    meta = jnp.stack(
        [
            targets.astype(f32),
            0.25 + 0.75 * groups.astype(f32),
            game_ids[:, :, 0].astype(f32),
            actions.astype(f32),
        ],
        axis=2,
    ).reshape(samples, 4)
    meta = jnp.pad(meta, ((0, 0), (0, 124))).astype(bf16)
    sent = jnp.swapaxes(pooled.reshape(samples, net.ns, col_width), 0, 1)
    sent = jnp.concatenate([sent, jnp.broadcast_to(meta[None], (net.ns, samples, 128))], axis=2)
    sent = jnp.broadcast_to(sent[None], (net.dp,) + sent.shape)
    feats = lax.all_to_all(
        sent.reshape(devices, samples, col_width + 128), ("dp", "ns"), 0, 0, tiled=True
    ).reshape(everyone, col_width + 128)
    feat_rows, logits, meta_slots, select = pl.pallas_call(
        functools.partial(head_in_kernel, col_width),
        name="head_in",
        in_specs=[SMEM] + [pl.BlockSpec(memory_space=pltpu.VMEM)] * 2,
        out_shape=[
            sds(slots, col_width, bf16),
            sds(slots, HPAD, f32),
            sds(slots, 128, f32),
            sds(everyone, slots, bf16),
        ],
        compiler_params=pltpu.CompilerParams(vmem_limit_bytes=48 * MIB),
    )(pos, feats, head)
    weight_total = jnp.sum(feats[:, col_width + 1].astype(f32))
    logits = net.add_all(logits, ("ns",))
    grad_low, back, loss = plain_call(
        head_loss_kernel,
        "head_loss",
        [sds(slots, HPAD, bf16), sds(everyone, col_width, bf16), sds(8, 128, f32)],
        [pltpu.VMEM((slots, HPAD), f32)],
    )(logits, meta_slots, head, select)
    returned = lax.all_to_all(
        back.reshape(devices, samples, col_width), ("dp", "ns"), 0, 0, tiled=True
    ).reshape(net.dp, net.ns, samples, col_width)
    grad_pooled = jnp.sum(returned.astype(f32), axis=0)
    grad_pooled = jnp.swapaxes(grad_pooled, 0, 1).reshape(samples // FPB, FPB, C) * (1.0 / PIX)
    grad_stream = jnp.pad(grad_pooled, ((0, 0), (0, 8 - FPB), (0, 0))).reshape(-1, C)

    def tail_back(layer, grad):
        x, xh1, rs1, taps, u2, xh2, rs2, xh3, rs3 = kept[layer]
        return run_tail_back(
            pos, grad, x, xh3, rs3, xh2, rs2, gains, lasts[layer], layer, layer == BLOCKS - 1
        )

    def conv_back(layer, da2, r):
        xh1, rs1 = kept[layer][1:3]
        one = ones[layer] if layer > 0 else None
        return run_conv_back(pos, da2, masks, xh1, rs1, gains, mids[layer], one, r, layer)

    shares, grams = {}, []

    def reduce_and_gram(ids, grads):
        got = yield from reduce_steps(net, pos, grads)
        got = dict(zip(ids, got, strict=True))
        *packs, share = cross_grams(pos, moms, got)
        shares[tuple(ids)] = share
        grams.append((tuple(ids), (yield from gram_steps(net, packs))))

    r, da3, da2, gacc3, gacc2 = tail_back(1, grad_stream)
    sum_a = Run(reduce_and_gram((5,), [weight_grad(kept[1][3], da2)]))
    sum_o = Run(gram_steps(net, old))
    sent = sum_a.step()
    da1, gacc1, grad_stream = conv_back(1, after(da2, *sent), r)
    gains_1 = jnp.concatenate([gacc1[:2], gacc2[:2], gacc3[:2]], axis=1)
    sent = sum_a.step(da1)
    grad_one, grad_last = weight_grad(x1, after(da1, *sent)), weight_grad(da3, kept[1][4])
    sum_b = Run(reduce_and_gram((2, 3), [grad_one, grad_last]))
    sent = sent + sum_b.step()
    r, da3, da2, gacc3, gacc2 = tail_back(0, after(grad_stream, *sent))
    sent = sum_b.step(da2) + sum_a.step(da2)
    sum_c = Run(reduce_and_gram((4,), [weight_grad(after(kept[0][3], *sent), da2)]))
    sent = sum_c.step() + sum_o.step()
    da1, gacc1 = conv_back(0, after(da2, *sent), None)

    grad_low = lax.dot_general(
        widen, after(grad_low, da1), (((1,), (1,)), ((), ())), preferred_element_type=f32
    ).astype(bf16)
    head_grad = jnp.dot(grad_low, feat_rows, preferred_element_type=f32)
    head_sq = jnp.sum(jnp.square(head_grad))
    head_grad = head_grad.reshape(HOUT, 1, col_width)
    loss_part = jnp.where(ns_idx == 0, loss[0, 0], 0.0)
    gains_0 = jnp.concatenate([gacc1[:2], gacc2[:2], gacc3[:2]], axis=1)
    small = jnp.stack([gains_0, gains_1]).reshape(-1, 1024)
    tail = jnp.zeros((16 - small.shape[0], 1024), f32)
    lane = jnp.arange(1024, dtype=jnp.int32)[None, :]
    tail = tail + jnp.where(lane == 0, loss_part, 0.0) + jnp.where(lane == 1, head_sq, 0.0)
    sum_s = Run(add_steps(net, jnp.concatenate([small, tail], axis=0)))

    sent = sum_c.step(da1) + sum_b.step(da1) + sum_a.step(da1)
    grad_one, grad_last = weight_grad(x0, after(da1, *sent)), weight_grad(after(da3, da1), kept[0][4])
    sum_d = Run(reduce_and_gram((0, 1), [grad_one, grad_last]))

    runs = (sum_d, sum_c, sum_b, sum_a, sum_s, sum_o)
    deps = (grad_one, grad_last)
    while not all(run.done for run in runs):
        sent = ()
        for run in runs:
            sent = sent + run.step(*deps)
        if sum_s.done:
            sent = sent + (sum_s.value,)
        deps = sent

    groups = tuple(ids for ids, _ in grams)
    gain_sum = sum_s.value[:12].reshape(BLOCKS, 2, 2 * MID + C)
    loss_sum, head_total = sum_s.value[12, 0], sum_s.value[12, 1]

    facts = jnp.stack([head_total + jnp.sum(jnp.square(gain_sum)), weight_total])
    pair_new, spatial_new, pair_moment, spatial_moment, report = newton(
        pos,
        facts,
        sum_o.value,
        groups,
        [got for _, got in grams],
        [w_pair.reshape(-1, MID), w_spatial.reshape(-1, MID)],
        moms,
        [shares[ids] for ids in groups],
    )
    grad_norm, factor = report[0, 0], report[0, 1]

    heads = heads_step(
        factor,
        [jnp.transpose(v, (2, 0, 1)) for v in (head_table, head_first, head_second)] + [head_grad],
    )
    heads = [jnp.transpose(v, (1, 2, 0)) for v in heads]
    norm_new, norm_first_new, norm_second_new = adam_step(
        norm_params, norm_first, norm_second, factor * gain_sum, rate_gain, 0.0
    )

    return (
        pair_new.reshape(w_pair.shape),
        spatial_new.reshape(w_spatial.shape),
        pair_moment.reshape(w_pair.shape),
        spatial_moment.reshape(w_spatial.shape),
        *heads,
        norm_new,
        norm_first_new,
        norm_second_new,
        grad_norm,
        loss_sum,
        weight_total,
    )


def solution(mesh):
    net = Net(mesh.shape["dp"], mesh.shape["ns"])
    samples = P(None, ("dp", "ns"))
    heads = P("dp", "ns", None)
    pairs, spatial = P(None, None, "ns", None), P(None, "ns", None)
    in_specs = (
        P(None, ("dp", "ns"), None, None),
        P(None, ("dp", "ns"), None),
        samples,
        samples,
        samples,
        pairs,
        spatial,
        pairs,
        spatial,
        heads,
        heads,
        heads,
        P(),
        P(),
        P(),
    )
    out_specs = (pairs, spatial, pairs, spatial, heads, heads, heads) + (P(),) * 6
    return jax.shard_map(
        functools.partial(local, net),
        mesh=mesh,
        in_specs=in_specs,
        out_specs=out_specs,
        check_vma=False,
    )
```

```python
import functools
import math

import jax
import jax.numpy as jnp
import numpy as np
from jax import lax
from jax.experimental import pallas as pl
from jax.experimental.pallas import tpu as pltpu
from jax.sharding import PartitionSpec as P

C = 2048
MID = 512
ACTIONS = 18
ATOMS = 51
GROUPS = 32
SIDE = 11
PIX = SIDE * SIDE
BLOCKS = 2
MB = 2
STEP = 10
SEG = 64
HPAD = ACTIONS * SEG
HOUT = ACTIONS * ATOMS

bf16 = jnp.bfloat16
f32 = jnp.float32

eps_norm = 1e-05
decay_moment = 0.5
beta_second = 0.95
adam_eps = 1e-08
rate_muon = 0.2
decay_muon = 0.01
rate_head = 0.02
decay_head = 0.01
rate_gain = 0.05
clip_limit = 0.01
cql_alpha = 0.05
value_max = 3.0
coef_a = 3.4445
coef_b = -4.775
coef_c = 2.0315

FROWS = 128
FPB = 2
BROWS = FPB * FROWS
TAPS = [(dr, dc) for dr in (-1, 0, 1) for dc in (-1, 0, 1)]
MIB = 1024 * 1024


def tap_masks():
    pixel = np.arange(FROWS)
    row, col = pixel // SIDE, pixel % SIDE
    masks = [
        (pixel < PIX) & (row + dr >= 0) & (row + dr < SIDE) & (col + dc >= 0) & (col + dc < SIDE)
        for dr, dc in TAPS
    ]
    return np.repeat(np.stack(masks).astype(np.float32).reshape(9 * FROWS, 1), 128, axis=1)


class Net:
    def __init__(self, dp, ns):
        self.dp, self.ns = dp, ns
        self.ns_bits = [1 << i for i in range(ns.bit_length() - 1)]
        self.dp_bits = [1 << i for i in range(dp.bit_length() - 1)]
        self.plain = not (dp == 8 and ns == 4)

    def swap(self, value, axis, bit):
        pairs = []
        for d in range(self.dp):
            for n in range(self.ns):
                partner = (d ^ bit) * self.ns + n if axis == "dp" else d * self.ns + (n ^ bit)
                pairs.append((d * self.ns + n, partner))
        return lax.ppermute(value, ("dp", "ns"), pairs)

    def add_all(self, value, axes=("dp", "ns")):
        for axis in axes:
            for bit in self.dp_bits if axis == "dp" else self.ns_bits:
                value = value + self.swap(value, axis, bit)
        return value


def pick(value, index, axis):
    return lax.dynamic_index_in_dim(value, index, axis, keepdims=False)


def bit_of(index, shift):
    return lax.rem(lax.div(index, 1 << shift), 2)


def after(value, *deps):
    return lax.optimization_barrier((value,) + deps)[0]


class Run:
    def __init__(self, steps):
        self.steps, self.deps, self.done, self.value = steps, None, False, None

    def step(self, *deps):
        if self.done:
            return ()
        try:
            sent = self.steps.send(deps if self.deps else None)
            self.deps = True
            return tuple(sent)
        except StopIteration as end:
            self.done, self.value = True, end.value
            return ()


class Shards:
    def __init__(self, arrays, pieces):
        self.arrays, self.pieces = arrays, pieces


def own_half(own):
    core = bit_of(lax.axis_index("dp"), 0)
    return pick(own.reshape(2, own.shape[0] // 2, MID), core, 0)


def gather_direct(net, shard):
    own = shard.astype(bf16)
    if net.plain:
        return Run(at_once([Shards((lax.all_gather(own, "ns", axis=0, tiled=True),), None)]))
    return Run(gather_direct_steps(net, own))


def at_once(value):
    if value is None:
        yield ()
    return value


def gather_direct_steps(net, own):
    half = own_half(own)
    n = half.shape[0]
    got = tuple(net.swap(half, "ns", rel) for rel in (1, 2, 3))
    deps = yield (got[0],)
    got = tuple(after(v, *deps) for v in got)
    other = tuple(net.swap(v, "dp", 1) for v in got)
    deps = yield got
    pieces = [(0, 0, (0, None, 0, 2 * n), 2 * n)]
    for core in range(2):
        for rel in (1, 2, 3):
            pieces.append((core * 3 + rel, 0, (rel, core, 0, 2 * n), n))
    return [Shards((own,) + got + other, pieces)]


def gather_two(net, shards, *deps):
    owns = [v.astype(bf16) for v in shards]
    if net.plain:
        return Run(
            at_once([Shards((lax.all_gather(v, "ns", axis=0, tiled=True),), None) for v in owns])
        )
    return Run(gather_two_steps(net, owns, deps))


def gather_two_steps(net, owns, deps):
    halves = [own_half(v) for v in owns]
    sizes = [v.shape[0] // 2 for v in halves]
    rows = sum(sizes)
    sent = jnp.concatenate(
        [v[:n] for v, n in zip(halves, sizes, strict=True)]
        + [v[n:] for v, n in zip(halves, sizes, strict=True)],
        axis=0,
    )
    sent = after(sent, *deps) if deps else sent
    got_x, got_y = net.swap(sent, "ns", 1), net.swap(sent, "ns", 2)
    deps = yield (sent,)
    got_x, got_y = after(got_x, *deps), after(got_y, *deps)
    sent = got_x[:rows], got_y[rows:]
    got_a, got_b = net.swap(sent[0], "ns", 2), net.swap(sent[1], "ns", 1)
    other = net.swap(got_x, "dp", 1), net.swap(got_y, "dp", 1)
    deps = yield sent
    got_a, got_b = after(got_a, *deps), after(got_b, *deps)
    got = (got_x, got_y, got_a, got_b)
    other = other + (net.swap(got_a, "dp", 1), net.swap(got_b, "dp", 1))
    yield got
    out, start = [], 0
    for own, n in zip(owns, sizes, strict=True):
        pieces = [(0, 0, (0, None, 0, 4 * n), 4 * n)]
        for core in range(2):
            at = 1 + 4 * core
            for rel, k in ((1, at), (2, at + 1)):
                pieces.append((k, start, (rel, core, 0, 4 * n), n))
                pieces.append((k, rows + start, (rel, core, n, 4 * n), n))
            pieces.append((at + 2, start, (3, core, 0, 4 * n), n))
            pieces.append((at + 3, start, (3, core, n, 4 * n), n))
        out.append(Shards((own,) + got + other, pieces))
        start += n
    return out


def export_rows(shard, buffer, full, sems):
    if full is None:
        return lambda: None
    copy = pltpu.make_async_copy(buffer, full, sems.at[13])
    pl.when(pl.program_id(0) == 0)(copy.start)
    return lambda: pl.when(pl.program_id(0) == pl.num_programs(0) - 1)(copy.wait)


def row_copies(shard, refs, pos_ref, buffer, sems):
    if shard.pieces is None:
        return [pltpu.make_async_copy(refs[0], buffer, sems.at[0])]
    here, my_core = pos_ref[0], pos_ref[1]
    copies = []
    for q, (k, row, (rel, core, offset, each), n) in enumerate(shard.pieces):
        if core is None:
            place = here * each
        else:
            place = (here ^ rel) * each + (my_core ^ core) * (each // 2) + offset
        copies.append(
            pltpu.make_async_copy(
                refs[k].at[pl.ds(row, n)],
                buffer.at[pl.ds(pl.multiple_of(place, 16), n)],
                sems.at[q],
            )
        )
    return copies


def load_rows(shard, refs, pos_ref, buffer, sems):
    copies = row_copies(shard, refs, pos_ref, buffer, sems)
    for copy in copies:
        copy.start()
    for copy in copies:
        copy.wait()


def place_rows(shard, refs, pos_ref, full, buffer, sems):
    copies = row_copies(shard, refs, pos_ref, buffer, sems)
    out = pltpu.make_async_copy(buffer, full, sems.at[13])
    step = pl.program_id(0)

    @pl.when(step == 0)
    def _():
        for copy in copies:
            copy.start()

    @pl.when(step == 1)
    def _():
        for copy in copies:
            copy.wait()
        out.start()

    @pl.when(step == pl.num_programs(0) - 1)
    def _():
        out.wait()


class Share:
    def __init__(self, arrays, pieces):
        self.arrays, self.pieces = arrays, pieces

    def copies(self, refs, pos, buffer, start, sems, first):
        out = []
        for q, (k, row, core, path, n) in enumerate(self.pieces):
            if core is None:
                place = start + path * n
            else:
                place = start + ((pos[1] ^ core) * 2 + (pos[5] ^ path)) * n
                place = pl.multiple_of(place, 16)
            out.append(
                pltpu.make_async_copy(
                    refs[k].at[pl.ds(row, n)], buffer.at[pl.ds(place, n)], sems.at[first + q]
                )
            )
        return out


SMALL = pl.CostEstimate(flops=1024, bytes_accessed=1024, transcendentals=0)


def vmem_call(kernel, name, ins, outs):
    return pl.pallas_call(
        kernel,
        name=name,
        in_specs=[pl.BlockSpec(memory_space=pltpu.SMEM)]
        + [pl.BlockSpec(memory_space=pltpu.VMEM)] * (len(ins) - 1),
        out_shape=[jax.ShapeDtypeStruct(shape, bf16) for shape in outs],
        cost_estimate=SMALL,
        compiler_params=pltpu.CompilerParams(vmem_limit_bytes=24 * MIB),
    )(*ins)


def split_kernel(count, pos, *refs):
    grads, gots, (send_a, send_b, keep_a, keep_b) = refs[:count], refs[count : 2 * count], refs[2 * count :]
    core, x, y = pos[1], pos[3], pos[4]
    start = 0
    for g, got in zip(grads, gots, strict=True):
        rows = pl.ds(start, g.shape[4])
        start += g.shape[4]
        for j in range(2):
            send_a[j, rows] = g[j, 1 - x, core, 0] + got[j, 1 - x, 0]
            keep_a[j, rows] = g[j, x, core, 0] + got[j, x, 0]
            send_b[j, rows] = g[1 - y, j, core, 1] + got[1 - y, j, 1]
            keep_b[j, rows] = g[y, j, core, 1] + got[y, j, 1]


def turn_kernel(pos, keep_a, keep_b, got_a, got_b, send_a, send_b, rest_a, rest_b):
    x, y = pos[3], pos[4]
    send_a[...] = keep_a[1 - y] + got_a[1 - y]
    send_b[...] = keep_b[1 - x] + got_b[1 - x]
    rest_a[...] = keep_a[y] + got_a[y]
    rest_b[...] = keep_b[x] + got_b[x]


def half_kernel(pos, rest_a, rest_b, got_a, got_b, send, keep):
    @pl.when(pos[5] == 0)
    def _():
        send[...] = rest_b[...] + got_b[...]
        keep[...] = rest_a[...] + got_a[...]

    @pl.when(pos[5] == 1)
    def _():
        send[...] = rest_a[...] + got_a[...]
        keep[...] = rest_b[...] + got_b[...]


def reduce_steps(net, pos, grads, late=()):
    if net.plain:
        yield ()
        out = []
        for g in [*grads, *late]:
            share = lax.psum_scatter(g.astype(f32), "ns", scatter_dimension=0, tiled=True)
            out.append(Share((lax.psum(share, "dp").astype(bf16),), [(0, 0, None, 0, share.shape[0])]))
        return out
    core = pos[1]

    def start(some):
        some = [g.reshape(2, 2, 2, 2, g.shape[0] // 16, MID) for g in some]
        sent = [pick(g, 1 - core, 2) for g in some]
        return some, sent, [net.swap(v, "dp", 1) for v in sent]

    grads, sent, gots = start(grads)
    deps = yield tuple(sent)
    gots = [after(v, *deps) for v in gots]
    more, _, got_more = start(late)
    grads, gots = grads + more, gots + got_more
    sizes = [g.shape[4] for g in grads]
    n = sum(sizes)
    two, one = (2, n, MID), (n, MID)
    send_a, send_b, keep_a, keep_b = vmem_call(
        functools.partial(split_kernel, len(grads)), "split_sum", [pos, *grads, *gots], [two] * 4
    )
    got_a, got_b = net.swap(send_a, "ns", 1), net.swap(send_b, "ns", 2)
    deps = yield send_a, send_b
    got_a, got_b = after(got_a, *deps), after(got_b, *deps)
    send_a, send_b, rest_a, rest_b = vmem_call(
        turn_kernel, "turn_sum", [pos, keep_a, keep_b, got_a, got_b], [one] * 4
    )
    got_a, got_b = net.swap(send_a, "ns", 2), net.swap(send_b, "ns", 1)
    deps = yield send_a, send_b
    got_a, got_b = after(got_a, *deps), after(got_b, *deps)
    sent, kept = vmem_call(half_kernel, "half_sum", [pos, rest_a, rest_b, got_a, got_b], [one] * 2)
    got = net.swap(sent, "dp", 2)
    deps = yield (sent,)
    kept = kept + after(got, *deps)
    got = net.swap(kept, "dp", 4)
    deps = yield (kept,)
    kept = kept + after(got, *deps)
    given, kept_other = net.swap(kept, "dp", 2), net.swap(kept, "dp", 1)
    deps = yield (kept,)
    given = after(given, *deps)
    given_other = net.swap(given, "dp", 1)
    deps = yield (given,)
    kept_other, given_other = after(kept_other, *deps), after(given_other, *deps)
    out, start = [], 0
    for size in sizes:
        out.append(
            Share(
                (kept, given, kept_other, given_other),
                [(k, start, k // 2, k % 2, size) for k in range(4)],
            )
        )
        start += size
    return out


HALF = MID // 2
PACK = HALF + 32
PATH = PACK // 2


def gram_steps(net, packs):
    first, second = packs
    if net.plain:
        first, second = (lax.psum(v.astype(f32), "ns").astype(bf16) for v in packs)
        return first, second, net.swap(first, "dp", 1), net.swap(second, "dp", 1)
    got_a, got_b = net.swap(first, "ns", 1), net.swap(second, "ns", 2)
    deps = yield first, second
    first, second = first + after(got_a, *deps), second + after(got_b, *deps)
    got_a, got_b = net.swap(first, "ns", 2), net.swap(second, "ns", 1)
    deps = yield first, second
    first, second = first + after(got_a, *deps), second + after(got_b, *deps)
    other = net.swap(first, "dp", 1), net.swap(second, "dp", 1)
    deps = yield first, second
    return first, second, after(other[0], *deps), after(other[1], *deps)


def add_steps(net, value):
    for axis, bits in (("dp", net.dp_bits), ("ns", net.ns_bits)):
        for bit in bits:
            got = net.swap(value, axis, bit)
            deps = yield (value,)
            value = value + after(got, *deps)
    return value


def sigmoid(v):
    return 0.5 * jnp.tanh(0.5 * v) + 0.5


def group_sum(t, size):
    tiles = t.shape[1] // 128
    u = jnp.concatenate([t[:, j * 128 : (j + 1) * 128] for j in range(tiles)], axis=0)
    lane = lax.broadcasted_iota(jnp.int32, u.shape, 1)
    step = 1
    while step < size:
        u = u + jnp.where(
            (lane & step) == 0, pltpu.roll(u, 128 - step, 1), pltpu.roll(u, step, 1)
        )
        step *= 2
    return jnp.concatenate([u[8 * j : 8 * j + 8] for j in range(tiles)], axis=1)


class Norm:
    def __init__(self, ref, layer, part):
        self.ref, self.row, self.base = ref, 2 * layer, (0, MID, 2 * MID)[part]

    def row_of(self, row, lanes):
        return self.ref[row : row + 1, self.base + lanes.start : self.base + lanes.stop]

    def gain(self, lanes):
        return self.row_of(self.row, lanes)

    def bias(self, lanes):
        return self.row_of(self.row + 1, lanes)


def live_rows():
    return lax.broadcasted_iota(jnp.int32, (FROWS, 128), 0) < PIX


def norm_stats(st, size):
    sums = group_sum(st[...], size) * (1.0 / (PIX * size))
    mean = sums[0:FPB]
    spread = jnp.maximum(sums[FPB : 2 * FPB] - mean * mean, 0.0)
    return mean, lax.rsqrt(spread + eps_norm)


def add_stats(st, f, lanes, v):
    st[f : f + 1, lanes] = jnp.sum(v, axis=0, keepdims=True)
    st[FPB + f : FPB + f + 1, lanes] = jnp.sum(v * v, axis=0, keepdims=True)


def units(width):
    for j in range(width // 128):
        for f in range(FPB):
            yield f, pl.ds(f * FROWS, FROWS), slice(j * 128, (j + 1) * 128)


def first_step(body):
    pl.when(pl.program_id(0) == 0)(body)


def reduce_kernel(shard, also, layer, raw, pos, x, gains, *rest):
    gb = Norm(gains, layer, 0)
    n = len(shard.arrays)
    refs, rest = rest[:n], rest[n:]
    if raw:
        frames, x, rest = x, rest[0], rest[1:]
        for f in range(FPB):
            last = (f + 1) * FROWS
            x[last - 16 : last] = jnp.zeros((16, C), bf16)
            x[f * FROWS : f * FROWS + PIX] = frames[f]
    if also is not None:
        n = len(also.arrays)
        place_rows(also, rest[:n], pos, rest[n + 4], *rest[-2:])
        rest = rest[n : n + 4] + rest[n + 5 : -2]
    h, xh, rs, full, buf, sems, acc, st = rest

    @first_step
    def _():
        load_rows(shard, refs, pos, buf, sems)
        st[...] = jnp.zeros_like(st)

    finish = export_rows(shard, buf, full, sems)
    for j in range(MID // 256):
        lanes = slice(j * 256, (j + 1) * 256)
        a = jnp.dot(x[...], buf[:, lanes], preferred_element_type=f32)
        acc[:, lanes] = a
        for f in range(FPB):
            add_stats(st, f, lanes, a[f * FROWS : (f + 1) * FROWS])
    norm_out(acc, st, gb, h, xh, rs)
    finish()


def norm_out(acc, st, gb, h, xh, rs):
    mean, rstd = norm_stats(st, MID // GROUPS)
    rs[...] = jnp.zeros_like(rs)
    rs[0:FPB] = rstd
    live = live_rows()
    for f, rows, lanes in units(MID):
        v = jnp.where(live, (acc[rows, lanes] - mean[f : f + 1, lanes]) * rstd[f : f + 1, lanes], 0.0)
        xh[rows, lanes] = v.astype(bf16)
        v = v * gb.gain(lanes) + gb.bias(lanes)
        h[rows, lanes] = jnp.where(live, v * sigmoid(v), 0.0).astype(bf16)


def spread_taps(src, masks, taps):
    for f, rows, lanes in units(MID):
        v = src[rows, lanes].astype(f32)
        for k, (dr, dc) in enumerate(TAPS):
            shift = -(dr * SIDE + dc)
            t = v if shift == 0 else pltpu.roll(v, shift % FROWS, 0)
            t = t * masks[k * FROWS : (k + 1) * FROWS]
            taps[rows, k * MID + lanes.start : k * MID + lanes.stop] = t.astype(bf16)


def conv_kernel(shard, also, layer, pos, src, masks, gains, *rest):
    gb = Norm(gains, layer, 1)
    n = len(shard.arrays)
    refs, rest = rest[:n], rest[n:]
    if also is not None:
        n = len(also.arrays)
        place_rows(also, rest[:n], pos, rest[n + 5], *rest[-2:])
        rest = rest[n : n + 5] + rest[n + 6 : -2]
    taps, u2, xh, rs, full, buf, sems, acc, st = rest

    @first_step
    def _():
        load_rows(shard, refs, pos, buf, sems)
        st[...] = jnp.zeros_like(st)

    finish = export_rows(shard, buf, full, sems)
    spread_taps(src, masks, taps)
    for j in range(MID // 256):
        lanes = slice(j * 256, (j + 1) * 256)
        a = jnp.dot(taps[...], buf[:, lanes], preferred_element_type=f32)
        acc[:, lanes] = a
        for f in range(FPB):
            add_stats(st, f, lanes, a[f * FROWS : (f + 1) * FROWS])
    norm_out(acc, st, gb, u2, xh, rs)
    finish()


def expand_kernel(shard, layer, last, pos, u2, x, gains, *rest):
    gb = Norm(gains, layer, 2)
    n = len(shard.arrays)
    refs, (xh, rs, out, full, buf, sems, acc, st) = rest[:n], rest[n:]

    @first_step
    def _():
        load_rows(shard, refs, pos, buf, sems)
        st[...] = jnp.zeros_like(st)

    finish = export_rows(shard, buf, full, sems)
    for j in range(C // 256):
        lanes = slice(j * 256, (j + 1) * 256)
        a = lax.dot_general(
            u2[...], buf[lanes, :], (((1,), (1,)), ((), ())), preferred_element_type=f32
        )
        acc[:, lanes] = a
        for f in range(FPB):
            add_stats(st, f, lanes, a[f * FROWS : (f + 1) * FROWS])
    mean, rstd = norm_stats(st, C // GROUPS)
    rs[...] = jnp.zeros_like(rs)
    rs[0:FPB] = rstd
    if last:
        out[...] = jnp.zeros_like(out)
    live = live_rows()
    for f, rows, lanes in units(C):
        v = jnp.where(live, (acc[rows, lanes] - mean[f : f + 1, lanes]) * rstd[f : f + 1, lanes], 0.0)
        xh[rows, lanes] = v.astype(bf16)
        v = x[rows, lanes].astype(f32) + (v * gb.gain(lanes) + gb.bias(lanes))
        v = jnp.where(live, v * sigmoid(v), 0.0)
        if last:
            out[f : f + 1, lanes] = jnp.sum(v, axis=0, keepdims=True) * (1.0 / PIX)
        else:
            out[rows, lanes] = v.astype(bf16)
    finish()


def back_sums(st, f, lanes, dv, xhat, gain, gacc):
    by_gain = jnp.sum(dv * xhat, axis=0, keepdims=True)
    by_bias = jnp.sum(dv, axis=0, keepdims=True)
    st[f : f + 1, lanes] = by_bias * gain
    st[FPB + f : FPB + f + 1, lanes] = by_gain * gain
    gacc[0:1, lanes] += by_gain
    gacc[1:2, lanes] += by_bias


def back_norm(st, size):
    sums = group_sum(st[...], size) * (1.0 / (PIX * size))
    return sums[0:FPB], sums[FPB : 2 * FPB]


def act_back(acc, st, xh, rs, gb, gacc, out):
    live = live_rows()
    for f, rows, lanes in units(MID):
        xhat = xh[rows, lanes].astype(f32)
        v = xhat * gb.gain(lanes) + gb.bias(lanes)
        s = sigmoid(v)
        dv = jnp.where(live, acc[rows, lanes] * (s + v * s * (1.0 - s)), 0.0)
        acc[rows, lanes] = dv
        back_sums(st, f, lanes, dv, xhat, gb.gain(lanes), gacc)
    m1, m2 = back_norm(st, MID // GROUPS)
    for f, rows, lanes in units(MID):
        xhat = xh[rows, lanes].astype(f32)
        da = rs[f : f + 1, lanes] * (
            acc[rows, lanes] * gb.gain(lanes) - m1[f : f + 1, lanes] - xhat * m2[f : f + 1, lanes]
        )
        out[rows, lanes] = jnp.where(live, da, 0.0).astype(bf16)


def tail_back_kernel(shard, layer, last, pos, d, x, xh3, rs3, xh2, rs2, gains, *rest):
    gb3, gb2 = Norm(gains, layer, 2), Norm(gains, layer, 1)
    n = len(shard.arrays)
    refs, (r, da3, da2, gacc3, gacc2, buf, sems, acc, st, acc2, st2) = rest[:n], rest[n:]

    @first_step
    def _():
        load_rows(shard, refs, pos, buf, sems)
        st[...] = jnp.zeros_like(st)
        st2[...] = jnp.zeros_like(st2)
        gacc3[...] = jnp.zeros_like(gacc3)
        gacc2[...] = jnp.zeros_like(gacc2)

    live = live_rows()
    for f, rows, lanes in units(C):
        xhat = xh3[rows, lanes].astype(f32)
        v = x[rows, lanes].astype(f32) + (xhat * gb3.gain(lanes) + gb3.bias(lanes))
        s = sigmoid(v)
        grad = d[f : f + 1, lanes] if last else d[rows, lanes].astype(f32)
        dv = jnp.where(live, grad * (s + v * s * (1.0 - s)), 0.0)
        acc[rows, lanes] = dv
        r[rows, lanes] = dv.astype(bf16)
        back_sums(st, f, lanes, dv, xhat, gb3.gain(lanes), gacc3)
    m1, m2 = back_norm(st, C // GROUPS)
    for f, rows, lanes in units(C):
        xhat = xh3[rows, lanes].astype(f32)
        da = rs3[f : f + 1, lanes] * (
            acc[rows, lanes] * gb3.gain(lanes) - m1[f : f + 1, lanes] - xhat * m2[f : f + 1, lanes]
        )
        da3[rows, lanes] = jnp.where(live, da, 0.0).astype(bf16)
    for j in range(MID // 256):
        lanes = slice(j * 256, (j + 1) * 256)
        acc2[:, lanes] = jnp.dot(da3[...], buf[:, lanes], preferred_element_type=f32)
    act_back(acc2, st2, xh2, rs2, gb2, gacc2, da2)


def conv_back_kernel(shard, shard_one, layer, pos, da2, masks, xh1, rs1, gains, *rest):
    gb1 = Norm(gains, layer, 0)
    n = len(shard.arrays)
    refs, rest = rest[:n], rest[n:]
    if shard_one is not None:
        n = len(shard_one.arrays)
        refs_one, (r, da1, gacc1, d, buf, sems, taps, acc, st, buf_one, sems_one) = rest[:n], rest[n:]
    else:
        da1, gacc1, buf, sems, taps, acc, st = rest

    @first_step
    def _():
        load_rows(shard, refs, pos, buf, sems)
        if shard_one is not None:
            load_rows(shard_one, refs_one, pos, buf_one, sems_one)
        st[...] = jnp.zeros_like(st)
        gacc1[...] = jnp.zeros_like(gacc1)

    spread_taps(da2, masks, taps)
    for j in range(MID // 256):
        total = None
        for k in range(9):
            part = lax.dot_general(
                taps[:, (8 - k) * MID : (9 - k) * MID],
                buf[k * MID + j * 256 : k * MID + (j + 1) * 256, :],
                (((1,), (1,)), ((), ())),
                preferred_element_type=f32,
            )
            total = part if total is None else total + part
        acc[:, j * 256 : (j + 1) * 256] = total
    act_back(acc, st, xh1, rs1, gb1, gacc1, da1)
    if shard_one is not None:
        for j in range(C // 256):
            lanes = slice(j * 256, (j + 1) * 256)
            a = lax.dot_general(
                da1[...], buf_one[lanes, :], (((1,), (1,)), ((), ())), preferred_element_type=f32
            )
            d[:, lanes] = (r[:, lanes].astype(f32) + a).astype(bf16)


def rows_spec(width):
    return pl.BlockSpec((BROWS, width), lambda i: (i, 0))


def eight_spec(width):
    return pl.BlockSpec((8, width), lambda i: (i, 0))


def gains_spec():
    return whole_spec(2 * BLOCKS, 2 * MID + C)


def whole_spec(rows, width):
    return pl.BlockSpec((rows, width), lambda i: (0, 0))


HBM = pl.BlockSpec(memory_space=pltpu.HBM)
ANY = pl.BlockSpec(memory_space=pl.ANY)
SMEM = pl.BlockSpec(memory_space=pltpu.SMEM)


def kept_sds(rows, width, dtype):
    return pltpu.HBM((rows, width), dtype)


def sds(rows, width, dtype):
    return jax.ShapeDtypeStruct((rows, width), dtype)


def call(kernel, name, rows, in_specs, outs, scratch, limit=48):
    return pl.pallas_call(
        kernel,
        name=name,
        grid=(rows // BROWS,),
        in_specs=in_specs,
        out_specs=[spec for _, spec in outs],
        out_shape=[shape for shape, _ in outs],
        scratch_shapes=scratch,
        cost_estimate=SMALL,
        compiler_params=pltpu.CompilerParams(
            vmem_limit_bytes=limit * MIB, dimension_semantics=("arbitrary",)
        ),
    )


def row_sems():
    return pltpu.SemaphoreType.DMA((14,))


def run_reduce(pos, x, shard, gains, layer, also=None):
    raw = x.ndim == 3
    rows = x.shape[0] * FROWS if raw else x.shape[0]
    more = also.arrays if also else ()
    eights = rows // BROWS * 8
    return call(
        functools.partial(reduce_kernel, shard, also, layer, raw),
        "reduce_norm",
        rows,
        [SMEM, pl.BlockSpec((FPB, PIX, C), lambda i: (i, 0, 0)) if raw else rows_spec(C), gains_spec()]
        + [ANY] * (len(shard.arrays) + len(more)),
        ([(kept_sds(rows, C, bf16), rows_spec(C))] if raw else [])
        + [
            (sds(rows, MID, bf16), rows_spec(MID)),
            (kept_sds(rows, MID, bf16), rows_spec(MID)),
            (kept_sds(eights, MID, f32), eight_spec(MID)),
            (kept_sds(C, MID, bf16), HBM),
        ]
        + ([(kept_sds(9 * MID, MID, bf16), HBM)] if also else []),
        [
            pltpu.VMEM((C, MID), bf16),
            row_sems(),
            pltpu.VMEM((BROWS, MID), f32),
            pltpu.VMEM((8, MID), f32),
        ]
        + ([pltpu.VMEM((9 * MID, MID), bf16), row_sems()] if also else []),
    )(pos, x, gains, *shard.arrays, *more)


def run_conv(pos, h, masks, shard, gains, layer, also=None):
    rows = h.shape[0]
    more = also.arrays if also else ()
    eights = rows // BROWS * 8
    return call(
        functools.partial(conv_kernel, shard, also, layer),
        "conv_norm",
        rows,
        [SMEM, rows_spec(MID), whole_spec(9 * FROWS, 128), gains_spec()]
        + [ANY] * (len(shard.arrays) + len(more)),
        [
            (kept_sds(rows, 9 * MID, bf16), rows_spec(9 * MID)),
            (sds(rows, MID, bf16), rows_spec(MID)),
            (kept_sds(rows, MID, bf16), rows_spec(MID)),
            (kept_sds(eights, MID, f32), eight_spec(MID)),
            (kept_sds(9 * MID, MID, bf16), HBM),
        ]
        + ([(kept_sds(C, MID, bf16), HBM)] if also else []),
        [
            pltpu.VMEM((9 * MID, MID), bf16),
            row_sems(),
            pltpu.VMEM((BROWS, MID), f32),
            pltpu.VMEM((8, MID), f32),
        ]
        + ([pltpu.VMEM((C, MID), bf16), row_sems()] if also else []),
    )(pos, h, masks, gains, *shard.arrays, *more)


def run_expand(pos, u2, x, shard, gains, layer, last):
    rows = x.shape[0]
    eights = rows // BROWS * 8
    return call(
        functools.partial(expand_kernel, shard, layer, last),
        "expand_norm",
        rows,
        [SMEM, rows_spec(MID), rows_spec(C), gains_spec()] + [ANY] * len(shard.arrays),
        [
            (kept_sds(rows, C, bf16), rows_spec(C)),
            (kept_sds(eights, C, f32), eight_spec(C)),
            (sds(eights, C, f32), eight_spec(C)) if last else (sds(rows, C, bf16), rows_spec(C)),
            (kept_sds(C, MID, bf16), HBM),
        ],
        [
            pltpu.VMEM((C, MID), bf16),
            row_sems(),
            pltpu.VMEM((BROWS, C), f32),
            pltpu.VMEM((8, C), f32),
        ],
    )(pos, u2, x, gains, *shard.arrays)


def run_tail_back(pos, d, x, xh3, rs3, xh2, rs2, gains, shard, layer, last):
    rows = x.shape[0]
    return call(
        functools.partial(tail_back_kernel, shard, layer, last),
        "tail_back",
        rows,
        [
            SMEM,
            eight_spec(C) if last else rows_spec(C),
            rows_spec(C),
            rows_spec(C),
            eight_spec(C),
            rows_spec(MID),
            eight_spec(MID),
            gains_spec(),
        ]
        + [HBM] * len(shard.arrays),
        [
            (sds(rows, C, bf16), rows_spec(C)),
            (sds(rows, C, bf16), rows_spec(C)),
            (sds(rows, MID, bf16), rows_spec(MID)),
            (sds(8, C, f32), whole_spec(8, C)),
            (sds(8, MID, f32), whole_spec(8, MID)),
        ],
        [
            pltpu.VMEM((C, MID), bf16),
            row_sems(),
            pltpu.VMEM((BROWS, C), f32),
            pltpu.VMEM((8, C), f32),
            pltpu.VMEM((BROWS, MID), f32),
            pltpu.VMEM((8, MID), f32),
        ],
    )(pos, d, x, xh3, rs3, xh2, rs2, gains, *shard.arrays)


def run_conv_back(pos, da2, masks, xh1, rs1, gains, shard, shard_one, r, layer):
    rows = da2.shape[0]
    more = shard_one is not None
    extra = shard_one.arrays if more else ()
    return call(
        functools.partial(conv_back_kernel, shard, shard_one, layer),
        "conv_back",
        rows,
        [
            SMEM,
            rows_spec(MID),
            whole_spec(9 * FROWS, 128),
            rows_spec(MID),
            eight_spec(MID),
            gains_spec(),
        ]
        + [HBM] * (len(shard.arrays) + len(extra))
        + ([rows_spec(C)] if more else []),
        [
            (sds(rows, MID, bf16), rows_spec(MID)),
            (sds(8, MID, f32), whole_spec(8, MID)),
        ]
        + ([(sds(rows, C, bf16), rows_spec(C))] if more else []),
        [
            pltpu.VMEM((9 * MID, MID), bf16),
            row_sems(),
            pltpu.VMEM((BROWS, 9 * MID), bf16),
            pltpu.VMEM((BROWS, MID), f32),
            pltpu.VMEM((8, MID), f32),
        ]
        + ([pltpu.VMEM((C, MID), bf16), row_sems()] if more else []),
        28,
    )(pos, da2, masks, xh1, rs1, gains, *shard.arrays, *extra, *([r] if more else []))


def head_in_kernel(width, pos, feats, head, rows_out, logits, meta_out, select_out):
    everyone, slots = feats.shape[0], rows_out.shape[0]
    meta = feats[:, width : width + 128]
    match = meta[:, 2:3].astype(f32) == pos[2].astype(f32)
    ones = jnp.where(match, 1.0, 0.0)
    row = lax.broadcasted_iota(jnp.int32, (everyone, everyone), 0)
    col = lax.broadcasted_iota(jnp.int32, (everyone, everyone), 1)
    earlier = jnp.where(col < row, 1.0, 0.0).astype(bf16)
    place = jnp.dot(
        earlier,
        jnp.broadcast_to(ones, (everyone, 128)).astype(bf16),
        preferred_element_type=f32,
    )[:, 0:1]
    slot = lax.broadcasted_iota(jnp.int32, (everyone, slots), 1).astype(f32)
    select = jnp.where((slot == place) & match, 1.0, 0.0).astype(bf16)
    select_out[...] = select
    turn = (((0,), (0,)), ((), ()))
    rows = lax.dot_general(select, feats[:, :width], turn, preferred_element_type=f32).astype(bf16)
    rows_out[...] = rows
    meta_out[...] = lax.dot_general(select, meta, turn, preferred_element_type=f32)
    logits[...] = jnp.dot(rows, head[...], preferred_element_type=f32)


def head_loss_kernel(logits, meta, head, select, grad_out, back, loss, probs):
    count = logits.shape[0]
    lane = lax.broadcasted_iota(jnp.int32, (count, 128), 1)
    spot = lane & (SEG - 1)
    level = value_max * (spot.astype(f32) * (2.0 / (ATOMS - 1)) - 1.0)
    values = jnp.zeros((count, 128), f32)
    columns = []
    for a in range(ACTIONS):
        chunk = slice(a // 2 * 128, a // 2 * 128 + 128)
        inside = (lane >= (a % 2) * SEG) & (lane < (a % 2) * SEG + ATOMS)
        v = logits[:, chunk]
        top = jnp.max(jnp.where(inside, v, -3.0e38), axis=1, keepdims=True)
        e = jnp.where(inside, jnp.exp(jnp.minimum(v - top, 0.0)), 0.0)
        p = e / jnp.sum(e, axis=1, keepdims=True)
        q = jnp.sum(p * level, axis=1, keepdims=True)
        columns.append(q)
        values = jnp.where(lane == a, q, values)
        if a % 2 == 0:
            probs[:, chunk] = p
        else:
            probs[:, chunk] += p
    target, weight, action = meta[:, 0:1], meta[:, 1:2], meta[:, 3:4]
    real = lane < ACTIONS
    hot = (lane.astype(f32) == action).astype(f32)
    chosen = jnp.sum(values * hot, axis=1, keepdims=True)
    top = jnp.max(jnp.where(real, values, -3.0e38), axis=1, keepdims=True)
    e = jnp.where(real, jnp.exp(jnp.minimum(values - top, 0.0)), 0.0)
    total = jnp.sum(e, axis=1, keepdims=True)
    soft_top = top + jnp.log(total)
    row_loss = weight * ((chosen - target) * (chosen - target) + cql_alpha * (soft_top - chosen))
    loss[...] = jnp.zeros(loss.shape, f32) + jnp.sum(row_loss, axis=0, keepdims=True)
    slope = weight * (2.0 * (chosen - target) * hot + cql_alpha * (e / total - hot))
    for j in range(ACTIONS // 2):
        chunk = slice(j * 128, j * 128 + 128)
        low = lane < SEG
        q = jnp.where(low, columns[2 * j], columns[2 * j + 1])
        s = jnp.where(low, slope[:, 2 * j : 2 * j + 1], slope[:, 2 * j + 1 : 2 * j + 2])
        grad_out[:, chunk] = (s * probs[:, chunk] * (level - q)).astype(bf16)
    feat = lax.dot_general(
        grad_out[...], head[...], (((1,), (1,)), ((), ())), preferred_element_type=f32
    ).astype(bf16)
    back[...] = jnp.dot(select[...], feat, preferred_element_type=f32).astype(bf16)


def plain_call(kernel, name, outs, scratch, limit=48):
    return pl.pallas_call(
        kernel,
        name=name,
        out_shape=outs,
        scratch_shapes=scratch,
        compiler_params=pltpu.CompilerParams(vmem_limit_bytes=limit * MIB),
    )


def adam_step(weight, first, second, grad_in, rate, decay):
    first_new = decay_moment * first + (1.0 - decay_moment) * grad_in
    second_new = beta_second * second + (1.0 - beta_second) * grad_in * grad_in
    normed = (
        first_new
        / (1.0 - decay_moment**STEP)
        / (jnp.sqrt(second_new / (1.0 - beta_second**STEP)) + adam_eps)
    )
    return (weight - rate * (normed + decay * weight), first_new, second_new)


def heads_kernel(factor, weight, first, second, grad, *outs):
    values = adam_step(
        weight[...], first[...], second[...], factor[0] * grad[...], rate_head, decay_head
    )
    for out, value in zip(outs, values, strict=True):
        out[...] = value


def heads_step(factor, arrays):
    width = arrays[0].shape[2]
    spec = pl.BlockSpec((HOUT // 6, 1, width), lambda i: (i, 0, 0))
    return pl.pallas_call(
        heads_kernel,
        name="heads",
        grid=(6,),
        in_specs=[SMEM] + [spec] * 4,
        out_specs=[spec] * 3,
        out_shape=[jax.ShapeDtypeStruct((HOUT, 1, width), f32)] * 3,
        compiler_params=pltpu.CompilerParams(vmem_limit_bytes=63 * MIB),
    )(factor.reshape(1), *arrays)


def gram(a, b):
    return jnp.einsum("ri,rj->ij", a, b, preferred_element_type=f32)


def weight_grad(a, b):
    return jnp.einsum("ri,rj->ij", a, b, preferred_element_type=f32).astype(bf16)


TURN = (((0,), (0,)), ((), ()))


def turned_dot(a, b):
    return lax.dot_general(a, b, TURN, preferred_element_type=f32)


def pack_to(out_a, out_b, slot, core, upper, lower):
    row = lax.broadcasted_iota(jnp.int32, (HALF, MID), 0) + core * HALF
    col = lax.broadcasted_iota(jnp.int32, (HALF, MID), 1)
    body = jnp.where(row < col, upper, lower).astype(bf16)
    diag = jnp.sum(jnp.where(row == col, upper, 0.0), axis=0, keepdims=True)
    out_a[slot] = body[:PATH]
    out_b[slot, : HALF - PATH] = body[PATH:]
    out_b[slot, HALF - PATH :] = jnp.broadcast_to(diag, (PACK - HALF, MID)).astype(bf16)


def rows_of(ref, k):
    n = ref.shape[0] // 4 if k < 4 else ref.shape[0] // 2
    return ref.at[pl.ds((k if k < 4 else k - 4) * n, n)], n


def core_columns(core):
    return pl.ds(pl.multiple_of(core * HALF, HALF), HALF)


def old_gram_kernel(pos, pair, spatial, out_a, out_b, buf, low, sems):
    core = pos[1]
    mine = core_columns(core)
    copies, spans, at = [], [], 0
    for k in range(6):
        src, n = rows_of(pair if k < 4 else spatial, k)
        spans.append(slice(at, at + n))
        copies.append(pltpu.make_async_copy(src, buf.at[pl.ds(at, n)], sems.at[k]))
        at += n
    for copy in copies:
        copy.start()
    for k in range(6):
        copies[k].wait()
        low[spans[k]] = buf[spans[k]].astype(bf16)
    for p in range(3):
        upper, lower = (turned_dot(low[spans[k], mine], low[spans[k]]) for k in (2 * p, 2 * p + 1))
        pack_to(out_a, out_b, p, core, upper, lower)


def cross_gram_kernel(shares, pos, pair, spatial, *rest):
    refs, (out_a, out_b, full, buf, share, low, sems) = rest[:-7], rest[-7:]
    core = pos[1]
    mine = core_columns(core)
    copies, spans, at, used = [], [], 0, 0
    for s, (k, got) in enumerate(shares.items()):
        src, n = rows_of(pair if k < 4 else spatial, k)
        spans.append(slice(at, at + n))
        group = [pltpu.make_async_copy(src, buf.at[pl.ds(at, n)], sems.at[5 * s])]
        here = refs[used : used + len(got.arrays)]
        used += len(got.arrays)
        group += got.copies(here, pos, share, at, sems, 5 * s + 1)
        copies.append(group)
        at += n
    for group in copies:
        for copy in group:
            copy.start()
    for s, span in enumerate(spans):
        for copy in copies[s]:
            copy.wait()
        if s == len(spans) - 1:
            export = pltpu.make_async_copy(share, full, sems.at[5 * len(spans)])
            export.start()
        low[span] = buf[span].astype(bf16)
        upper = turned_dot(low[span, mine], share[span]) + turned_dot(share[span, mine], low[span])
        pack_to(out_a, out_b, s, core, upper, turned_dot(share[span, mine], share[span]))
    export.wait()


def gram_call(kernel, name, pos, moms, arrays, rows, count, scratch, sems, outs=()):
    return pl.pallas_call(
        kernel,
        name=name,
        in_specs=[SMEM, HBM, HBM] + [ANY] * len(arrays),
        out_specs=[pl.BlockSpec(memory_space=pltpu.VMEM)] * 2 + [HBM] * len(outs),
        out_shape=[jax.ShapeDtypeStruct((count, PATH, MID), bf16)] * 2 + list(outs),
        scratch_shapes=[pltpu.VMEM((rows, MID), f32)]
        + [pltpu.VMEM((rows, MID), bf16)] * scratch
        + [pltpu.SemaphoreType.DMA((sems,))],
        cost_estimate=SMALL,
        compiler_params=pltpu.CompilerParams(vmem_limit_bytes=63 * MIB),
    )(pos, *moms, *arrays)


def old_grams(pos, moms):
    rows = moms[0].shape[0] + moms[1].shape[0]
    return gram_call(old_gram_kernel, "old_gram", pos, moms, [], rows, 3, 1, 6)


def cross_grams(pos, moms, shares):
    rows = sum(moms[0].shape[0] // 4 if k < 4 else moms[1].shape[0] // 2 for k in shares)
    return gram_call(
        functools.partial(cross_gram_kernel, shares),
        "cross_gram",
        pos,
        moms,
        [v for share in shares.values() for v in share.arrays],
        rows,
        len(shares),
        2,
        5 * len(shares) + 1,
        [kept_sds(rows, MID, bf16)],
    )


def newton_kernel(groups, pos, facts, *rest):
    counts, order = tuple(len(g) for g in groups), [k for g in groups for k in g]
    n = 4 * (1 + len(counts))
    packs, rest = rest[:n], rest[n:]
    weights, moms, rest = rest[0:2], rest[2:4], rest[4:]
    shares, rest = rest[: len(groups)], rest[len(groups) :]
    news, moments, report, rest = rest[0:2], rest[2:4], rest[4], rest[5:]
    olds, crosses, w_buf, m_buf, g_buf, poly, sems, big_sems, share_sems, out_sems = rest
    pair_rows, rows = weights[0].shape[0], w_buf.shape[0]
    core = pos[1]
    spans, at = [], 0
    for k in range(6):
        count = pair_rows // 4 if k < 4 else (rows - pair_rows) // 2
        spans.append((at, count))
        at += count

    small = []
    at = 0
    for q, count in enumerate((3,) + counts):
        buffer = olds if q == 0 else crosses
        for j in range(4):
            side = core if j < 2 else 1 - core
            small.append(
                pltpu.make_async_copy(
                    packs[4 * q + j],
                    buffer.at[side, pl.ds(at, count), pl.ds(j % 2 * PATH, PATH)],
                    sems.at[4 * q + j],
                )
            )
        at = 0 if q == 0 else at + count
    big = []
    for q, (src, dst) in enumerate(((weights, w_buf), (moms, m_buf))):
        big.append(pltpu.make_async_copy(src[0], dst.at[pl.ds(0, pair_rows)], big_sems.at[2 * q]))
        big.append(
            pltpu.make_async_copy(
                src[1], dst.at[pl.ds(pair_rows, rows - pair_rows)], big_sems.at[2 * q + 1]
            )
        )
    for ids, share in zip(groups, shares, strict=True):
        at = 0
        for k in ids:
            start, n = spans[k]
            big.append(
                pltpu.make_async_copy(
                    share.at[pl.ds(at, n)], g_buf.at[pl.ds(start, n)], share_sems.at[k]
                )
            )
            at += n
    for copy in small:
        copy.start()
    for copy in small:
        copy.wait()
    for copy in big:
        copy.start()

    row = lax.broadcasted_iota(jnp.int32, (MID, MID), 0)
    col = lax.broadcasted_iota(jnp.int32, (MID, MID), 1)
    above, on = row < col, row == col

    def total(v):
        return jnp.sum(jnp.sum(v, axis=0, keepdims=True), axis=1, keepdims=True)

    def pack_of(buffer, p):
        body = jnp.concatenate([buffer[0, p, 0:HALF], buffer[1, p, 0:HALF]], axis=0).astype(f32)
        diag = (
            buffer[0, p, HALF : HALF + 16].astype(f32) + buffer[1, p, HALF : HALF + 16].astype(f32)
        )
        return body, diag[0:1]

    def diag_of(body):
        return jnp.sum(jnp.where(on, body, 0.0), axis=0, keepdims=True)

    squares = jnp.zeros((1, 1), f32)
    for p in range(6):
        squares = squares + total(jnp.where(on, pack_of(crosses, p)[0], 0.0))
    weight_total = jnp.zeros((1, 1), f32) + facts[1]
    grad_norm = jnp.sqrt(squares + facts[0]) / weight_total
    factor = jnp.minimum(1.0, clip_limit / grad_norm) / weight_total
    lane = lax.broadcasted_iota(jnp.int32, report.shape, 1)
    report[...] = jnp.where(lane == 0, grad_norm, factor)

    def low_dot(a, b):
        return jnp.dot(a.astype(bf16), b.astype(bf16), preferred_element_type=f32)

    scales = []
    for k in range(6):
        old, old_diag = pack_of(olds, k // 2)
        body, cross_diag = pack_of(crosses, order.index(k))
        quarter, half_factor = decay_moment * decay_moment, decay_moment * factor
        if k % 2 == 0:
            part = jnp.where(above, quarter * old + half_factor * body, (factor * factor) * body)
        else:
            old_diag = diag_of(old)
            part = jnp.where(above, half_factor * body, quarter * old + (factor * factor) * body)
        diag = quarter * old_diag + half_factor * cross_diag + (factor * factor) * diag_of(body)
        part = jnp.where(on, 0.5 * diag, part)
        g = part + part.T
        frob = jnp.sqrt(jnp.maximum(jnp.sum(diag, axis=1, keepdims=True), 0.0))
        scale = 1.0 / (frob + 1e-07)
        scales.append(scale)
        g0 = g * (scale * scale)
        e1 = coef_b * g0 + coef_c * low_dot(g0, g0)
        h = coef_a * g0 + low_dot(g0, e1)
        g1 = coef_a * h + low_dot(h, e1)
        e2 = coef_b * g1 + coef_c * low_dot(g1, g1)
        poly[k] = (coef_a * (e1 + e2) + low_dot(e1, e2)).astype(bf16)

    for copy in big:
        copy.wait()
    outs = []
    for k in range(6):
        start, count = spans[k]
        gain = 0.2 * math.sqrt(C if k < 4 else 9 * MID)
        chunk = 256 if count % 256 == 0 else 128 if count % 128 == 0 else 32
        for j in range(count // chunk):
            here = slice(start + j * chunk, start + (j + 1) * chunk)
            moment = decay_moment * m_buf[here] + factor * g_buf[here].astype(f32)
            m_buf[here] = moment
            current = moment * scales[k]
            ortho = (coef_a * coef_a) * current + jnp.dot(
                current.astype(bf16), poly[k], preferred_element_type=f32
            )
            w_buf[here] = (1.0 - rate_muon * decay_muon) * w_buf[here] - (rate_muon * gain) * ortho
        which, base = (0, 0) if k < 4 else (1, pair_rows)
        for q, (buf, dst) in enumerate(((w_buf, news), (m_buf, moments))):
            copy = pltpu.make_async_copy(
                buf.at[pl.ds(start, count)],
                dst[which].at[pl.ds(start - base, count)],
                out_sems.at[2 * k + q],
            )
            copy.start()
            outs.append(copy)
    for copy in outs:
        copy.wait()


def newton(pos, facts, olds, groups, crosses, weights, moms, shares):
    rows = weights[0].shape[0] + weights[1].shape[0]
    packs = [v for group in (olds, *crosses) for v in group]
    return pl.pallas_call(
        functools.partial(newton_kernel, groups),
        name="newton",
        in_specs=[SMEM, SMEM]
        + [HBM] * len(packs)
        + [HBM] * (4 + len(shares)),
        out_specs=[HBM] * 4 + [pl.BlockSpec(memory_space=pltpu.VMEM)],
        out_shape=[jax.ShapeDtypeStruct(w.shape, f32) for w in weights] * 2 + [sds(8, 128, f32)],
        scratch_shapes=[
            pltpu.VMEM((2, 3, PACK, MID), bf16),
            pltpu.VMEM((2, 6, PACK, MID), bf16),
            pltpu.VMEM((rows, MID), f32),
            pltpu.VMEM((rows, MID), f32),
            pltpu.VMEM((rows, MID), bf16),
            pltpu.VMEM((6, MID, MID), bf16),
            pltpu.SemaphoreType.DMA((len(packs),)),
            pltpu.SemaphoreType.DMA((4,)),
            pltpu.SemaphoreType.DMA((6,)),
            pltpu.SemaphoreType.DMA((12,)),
        ],
        compiler_params=pltpu.CompilerParams(vmem_limit_bytes=63 * MIB),
    )(pos, facts, *packs, *weights, *moms, *shares)


def local(
    net,
    frames,
    game_ids,
    actions,
    groups,
    targets,
    w_pair,
    w_spatial,
    mom_pair,
    mom_spatial,
    head_table,
    head_first,
    head_second,
    norm_params,
    norm_first,
    norm_second,
):
    dp_idx, ns_idx = lax.axis_index("dp"), lax.axis_index("ns")
    pos = jnp.stack(
        [ns_idx, bit_of(dp_idx, 0), dp_idx, bit_of(ns_idx, 0), bit_of(ns_idx, 1), bit_of(dp_idx, 1)]
    ).astype(jnp.int32)
    dev_rows = frames.shape[1]
    samples = MB * dev_rows
    rows = samples * FROWS
    devices = net.dp * net.ns
    everyone = devices * samples
    slots = MB * net.dp * (2 * net.ns * dev_rows // net.dp)
    col_width = C // net.ns

    get_a = gather_direct(net, w_pair[0, 0])
    get_a.step()

    masks = jnp.asarray(tap_masks())
    frames = frames.reshape(samples, PIX, C)
    gains = norm_params.reshape(2 * BLOCKS, 2 * MID + C)
    got = get_a.step()
    get_b = gather_two(net, [w_spatial[0], w_pair[0, 1]], *got)
    sent = get_b.step()
    get_a.step()
    x0, h, xh1, rs1, one = run_reduce(pos, after(frames, *sent), get_a.value[0], gains, 0)
    sent = get_b.step(h)

    out_col = jnp.arange(HOUT, dtype=jnp.int32)
    widen = (
        (out_col // ATOMS * SEG + out_col % ATOMS)[:, None] == jnp.arange(HPAD, dtype=jnp.int32)
    ).astype(bf16)
    head = jnp.dot(after(head_table, *sent)[0].astype(bf16), widen, preferred_element_type=f32).astype(bf16)

    moms = [mom_pair.reshape(-1, MID), mom_spatial.reshape(-1, MID)]
    old = old_grams(after(pos, *sent), moms)

    sent = sent + (*old, head)
    get_c = gather_two(net, [w_pair[1, 0], w_spatial[1]], *sent)
    sent = sent + get_c.step()
    get_b.step(*sent)
    get_b.step()
    kept = [(x0, xh1, rs1)]
    ones, mids, lasts = [one], [], []
    taps, u2, xh2, rs2, mid, last = run_conv(
        pos, h, masks, get_b.value[0], gains, 0, get_b.value[1]
    )
    sent = get_c.step(u2)
    get_d = gather_two(net, [w_pair[1, 1]], *sent)
    sent = get_d.step()
    xh3, rs3, x1, _ = run_expand(
        pos, after(u2, *sent), x0, Shards((last,), None), gains, 0, False
    )
    kept[0] = kept[0] + (taps, u2, xh2, rs2, xh3, rs3)
    mids.append(mid)
    lasts.append(last)
    get_c.step(x1)
    get_c.step()
    sent = get_d.step(x1)
    h, xh1, rs1, one, mid = run_reduce(
        pos, after(x1, *sent), get_c.value[0], gains, 1, get_c.value[1]
    )
    taps, u2, xh2, rs2, _ = run_conv(pos, h, masks, Shards((mid,), None), gains, 1)
    get_d.step(h)
    get_d.step()
    xh3, rs3, stream, last = run_expand(pos, u2, x1, get_d.value[0], gains, 1, True)
    kept.append((x1, xh1, rs1, taps, u2, xh2, rs2, xh3, rs3))
    ones, mids, lasts = [
        [Shards((v,), None) for v in pair]
        for pair in ((ones[0], one), (mids[0], mid), (lasts[0], last))
    ]
    pooled = stream.reshape(-1, 8, C)[:, :FPB].reshape(samples, C).astype(bf16)

    meta = jnp.stack(
        [
            targets.astype(f32),
            0.25 + 0.75 * groups.astype(f32),
            game_ids[:, :, 0].astype(f32),
            actions.astype(f32),
        ],
        axis=2,
    ).reshape(samples, 4)
    meta = jnp.pad(meta, ((0, 0), (0, 124))).astype(bf16)
    sent = jnp.swapaxes(pooled.reshape(samples, net.ns, col_width), 0, 1)
    sent = jnp.concatenate([sent, jnp.broadcast_to(meta[None], (net.ns, samples, 128))], axis=2)
    sent = jnp.broadcast_to(sent[None], (net.dp,) + sent.shape)
    feats = lax.all_to_all(
        sent.reshape(devices, samples, col_width + 128), ("dp", "ns"), 0, 0, tiled=True
    ).reshape(everyone, col_width + 128)
    feat_rows, logits, meta_slots, select = pl.pallas_call(
        functools.partial(head_in_kernel, col_width),
        name="head_in",
        in_specs=[SMEM] + [pl.BlockSpec(memory_space=pltpu.VMEM)] * 2,
        out_shape=[
            sds(slots, col_width, bf16),
            sds(slots, HPAD, f32),
            sds(slots, 128, f32),
            sds(everyone, slots, bf16),
        ],
        compiler_params=pltpu.CompilerParams(vmem_limit_bytes=48 * MIB),
    )(pos, feats, head)
    weight_total = jnp.sum(feats[:, col_width + 1].astype(f32))
    logits = net.add_all(logits, ("ns",))
    grad_low, back, loss = plain_call(
        head_loss_kernel,
        "head_loss",
        [sds(slots, HPAD, bf16), sds(everyone, col_width, bf16), sds(8, 128, f32)],
        [pltpu.VMEM((slots, HPAD), f32)],
    )(logits, meta_slots, head, select)
    returned = lax.all_to_all(
        back.reshape(devices, samples, col_width), ("dp", "ns"), 0, 0, tiled=True
    ).reshape(net.dp, net.ns, samples, col_width)
    grad_pooled = jnp.sum(returned.astype(f32), axis=0)
    grad_pooled = jnp.swapaxes(grad_pooled, 0, 1).reshape(samples // FPB, FPB, C) * (1.0 / PIX)
    grad_stream = jnp.pad(grad_pooled, ((0, 0), (0, 8 - FPB), (0, 0))).reshape(-1, C)

    def tail_back(layer, grad):
        x, xh1, rs1, taps, u2, xh2, rs2, xh3, rs3 = kept[layer]
        return run_tail_back(
            pos, grad, x, xh3, rs3, xh2, rs2, gains, lasts[layer], layer, layer == BLOCKS - 1
        )

    def conv_back(layer, da2, r):
        xh1, rs1 = kept[layer][1:3]
        one = ones[layer] if layer > 0 else None
        return run_conv_back(pos, da2, masks, xh1, rs1, gains, mids[layer], one, r, layer)

    shares, grams = {}, []

    def reduce_and_gram(ids, grads, late):
        got = yield from reduce_steps(net, pos, grads, late)
        got = dict(zip(ids, got, strict=True))
        *packs, share = cross_grams(pos, moms, got)
        shares[tuple(ids)] = share
        grams.append((tuple(ids), (yield from gram_steps(net, packs))))

    sum_o = Run(gram_steps(net, [after(v, grad_stream) for v in old]))
    r, da3, da2, gacc3, gacc2 = tail_back(1, after(grad_stream, *sum_o.step()))
    da2 = after(da2, *sum_o.step(da2))
    late_a, late_b = [], []
    grad_mid, grad_last = weight_grad(kept[1][3], da2), weight_grad(da3, kept[1][4])
    sum_a = Run(reduce_and_gram((5, 3, 2), [grad_mid, grad_last], late_a))
    sent = sum_a.step()
    sent = sent + sum_o.step(*sent)
    da1, gacc1, grad_stream = conv_back(1, after(da2, *sent), r)
    sum_o.step(da1)
    gains_1 = jnp.concatenate([gacc1[:2], gacc2[:2], gacc3[:2]], axis=1)
    late_a.append(weight_grad(x1, da1))
    sent = sum_a.step(da1)
    r, da3, da2, gacc3, gacc2 = tail_back(0, after(grad_stream, *sent))
    sent = sum_a.step(da2)
    grad_mid, grad_last = weight_grad(after(kept[0][3], *sent), da2), weight_grad(da3, kept[0][4])
    sum_b = Run(reduce_and_gram((4, 1, 0), [grad_mid, grad_last], late_b))
    sent = sum_b.step()
    sent = sent + sum_a.step(grad_mid, grad_last, *sent)
    da1, gacc1 = conv_back(0, after(da2, *sent), None)
    sent = sum_a.step(da1)
    late_b.append(weight_grad(x0, after(da1, *sent)))
    sent_b = sum_b.step(*sent, late_b[0])

    grad_low = lax.dot_general(
        widen, after(grad_low, *sent_b), (((1,), (1,)), ((), ())), preferred_element_type=f32
    ).astype(bf16)
    head_grad = jnp.dot(grad_low, feat_rows, preferred_element_type=f32)
    head_sq = jnp.sum(jnp.square(head_grad))
    head_grad = head_grad.reshape(HOUT, 1, col_width)
    loss_part = jnp.where(ns_idx == 0, loss[0, 0], 0.0)
    gains_0 = jnp.concatenate([gacc1[:2], gacc2[:2], gacc3[:2]], axis=1)
    small = jnp.stack([gains_0, gains_1]).reshape(-1, 1024)
    tail = jnp.zeros((16 - small.shape[0], 1024), f32)
    lane = jnp.arange(1024, dtype=jnp.int32)[None, :]
    tail = tail + jnp.where(lane == 0, loss_part, 0.0) + jnp.where(lane == 1, head_sq, 0.0)
    small = after(jnp.concatenate([small, tail], axis=0), head_grad, weight_total)
    sum_s = Run(add_steps(net, small))

    runs = {"a": sum_a, "b": sum_b, "s": sum_s}
    sent = sent + sent_b
    def read_sums(value):
        gain_sum = value[:12].reshape(BLOCKS, 2, 2 * MID + C)
        facts = jnp.stack([value[12, 1] + jnp.sum(jnp.square(gain_sum)), weight_total])
        return gain_sum, value[12, 0], facts

    sums = None
    for name in "assbabasbasbasbasbbbb":
        sent = runs[name].step(*sent) or sent
        if sum_s.done and sums is None:
            sums = read_sums(sum_s.value)
            sent = sent + (sums[2],)
    while not all(run.done for run in runs.values()):
        for run in runs.values():
            sent = run.step(*sent) or sent
    gain_sum, loss_sum, facts = sums or read_sums(sum_s.value)

    groups = tuple(ids for ids, _ in grams)
    pair_new, spatial_new, pair_moment, spatial_moment, report = newton(
        pos,
        facts,
        sum_o.value,
        groups,
        [got for _, got in grams],
        [w_pair.reshape(-1, MID), w_spatial.reshape(-1, MID)],
        moms,
        [shares[ids] for ids in groups],
    )
    grad_norm, factor = report[0, 0], report[0, 1]

    heads = heads_step(
        factor,
        [jnp.transpose(v, (2, 0, 1)) for v in (head_table, head_first, head_second)] + [head_grad],
    )
    heads = [jnp.transpose(v, (1, 2, 0)) for v in heads]
    norm_new, norm_first_new, norm_second_new = adam_step(
        norm_params, norm_first, norm_second, factor * gain_sum, rate_gain, 0.0
    )

    return (
        pair_new.reshape(w_pair.shape),
        spatial_new.reshape(w_spatial.shape),
        pair_moment.reshape(w_pair.shape),
        spatial_moment.reshape(w_spatial.shape),
        *heads,
        norm_new,
        norm_first_new,
        norm_second_new,
        grad_norm,
        loss_sum,
        weight_total,
    )


def solution(mesh):
    net = Net(mesh.shape["dp"], mesh.shape["ns"])
    samples = P(None, ("dp", "ns"))
    heads = P("dp", "ns", None)
    pairs, spatial = P(None, None, "ns", None), P(None, "ns", None)
    in_specs = (
        P(None, ("dp", "ns"), None, None),
        P(None, ("dp", "ns"), None),
        samples,
        samples,
        samples,
        pairs,
        spatial,
        pairs,
        spatial,
        heads,
        heads,
        heads,
        P(),
        P(),
        P(),
    )
    out_specs = (pairs, spatial, pairs, spatial, heads, heads, heads) + (P(),) * 6
    return jax.shard_map(
        functools.partial(local, net),
        mesh=mesh,
        in_specs=in_specs,
        out_specs=out_specs,
        check_vma=False,
    )
```
